512 devices in a mesh: rep: 8 (over y_hi, x), shard: 64 (over z, y_lo, core).
Axes of the slice: x: 4, y: 8 (y_hi: 2, y_lo: 4; y = y_hi * 4 + y_lo), z: 8, core: 2. Of those that a mesh axis runs over, the one named last changes fastest.
Arguments:
- hidden: bfloat16 [196608, 768], P(('rep', 'shard')), may hold values from -24 to 24
- prob: float32 [196608], P(('rep', 'shard')), may hold values from 0.05 to 0.5
- counts: int32 [512], P(('rep', 'shard')), may hold values from 96 to 384, as said below
- down_weight: bfloat16 [768, 2048], P('shard'), may hold values from -0.21875 to 0.21875
- cotangent: bfloat16 [196608, 2048], P(('rep', 'shard')), may hold values from -0.59765625 to 0.59765625
Outputs:
- output: bfloat16 [196608, 2048], P(('rep', 'shard'))
- grad_hidden: bfloat16 [196608, 768], P(('rep', 'shard'))
- grad_prob: float32 [196608], P(('rep', 'shard'))
- grad_weight: float32 [768, 2048], P('shard')
The draws below stay inside these ranges and needn't reach their ends.
Inputs may be any that keep to these rules, and one draw needn't show every extreme that they name: Entry b counts the live rows at the start of block b of 384 slots; the rest of the block is padding; some block is full in every draw.
All inputs are finite; a program needn't handle non-finite values.
Results may differ from the reference program's by a relative error of at most 0.014.
Values may be sent and summed in bfloat16 or wider, within the bound.
A program may use at most 64 MiB of HBM per device.

```python
import jax
import jax.numpy as jnp
from jax import lax

D = 2048
FF = 768
CAP = 384
TOKENS = 196608


def draw_counts(key, part):
    key = jax.random.fold_in(key, 11)
    blocks = TOKENS // CAP
    values = jax.random.randint(key, (blocks,), CAP // 4, CAP + 1)
    chosen = jax.random.randint(jax.random.fold_in(key, 5), (), 0, blocks)
    return jnp.where(jnp.arange(blocks) == chosen, CAP, values).astype(jnp.int32)


def with_spikes(array, rng, source, target, shards_of, factor):
    owner, partner = [(jnp.arange(array.shape[dim]) // (array.shape[dim] // shards_of)).reshape([-1 if axis == dim else 1 for axis in range(array.ndim)]) for dim in (source, target)]
    chosen = jax.random.permutation(rng, shards_of)[partner]
    strong = (owner == chosen) | (owner == (partner + shards_of // 2) % shards_of)
    return jnp.where(strong, factor * array, array)


def shard_levels(stream_key, extent, shards, low, top_value):
    def one(dim, shards_of):
        steps = jax.random.uniform(jax.random.fold_in(jax.random.fold_in(stream_key, 6), dim), (shards_of,), jnp.float32, low / len(shards), top_value / len(shards))
        return jnp.repeat(jnp.exp(steps), extent[dim] // shards_of).reshape((-1,) + (1,) * (len(extent) - dim - 1))

    level = one(*shards[0])
    for cut in shards[1:]:
        level = level * one(*cut)
    return level


def bell_draw(key, dims, deviation, most, shards=(), kind=jnp.bfloat16):
    entries = deviation * jax.random.normal(key, dims, jnp.float32)
    if shards:
        entries = entries * shard_levels(key, dims, shards, -0.22, 0.18)
    return jnp.clip(entries, -most, most).astype(kind)


def noise_with(own_key, extent, deviation, reach, shards, heavy, kind=jnp.bfloat16):
    drawn = deviation * jax.random.normal(own_key, extent, jnp.float32)
    if shards:
        drawn = drawn * shard_levels(own_key, extent, shards, -0.22, 0.18)
    return jnp.clip(with_spikes(drawn, jax.random.fold_in(own_key, 3), *heavy), -reach, reach).astype(kind)


def setup_inputs(seed: int = 0) -> dict:
    key_of = jax.random.split(jax.random.key(seed), 6)
    hidden = noise_with(key_of[0], (TOKENS, FF), 1.0, 24.0, ((0, 512),), (0, 1, 256, 6.0))
    prob = jnp.clip(0.05 + 0.45 * jax.random.uniform(key_of[1], (TOKENS,), jnp.float32) ** shard_levels(key_of[1], (TOKENS,), ((0, 512),), -0.2, 0.2), 0.05, 0.5)
    counts = draw_counts(jax.random.fold_in(key_of[5], 71), 0)
    down_weight = bell_draw(key_of[3], (FF, D), FF ** -0.5, 0.21875, ((0, 64),))
    cotangent = bell_draw(key_of[4], (TOKENS, D), 0.1, 0.59765625, ((0, 512),))
    return {"hidden": hidden, "prob": prob, "counts": counts, "down_weight": down_weight, "cotangent": cotangent}


def reference(hidden, prob, counts, down_weight, cotangent):
    blocks = TOKENS // CAP
    hid_blocks = hidden.reshape(blocks, CAP, FF)
    prob_blocks = prob.reshape(blocks, CAP)
    cot_blocks = cotangent.reshape(blocks, CAP, D)

    def step(total, item):
        rows, weights, grads, number = item
        live = (jnp.arange(CAP, dtype=jnp.int32) < number).astype(jnp.float32)
        weight = weights * live
        proj = jnp.dot(rows, down_weight, preferred_element_type=jnp.float32)
        output = (weight[:, None] * proj).astype(jnp.bfloat16)
        scaled = (weight[:, None] * grads.astype(jnp.float32)).astype(jnp.bfloat16)
        grad_rows = lax.dot_general(scaled, down_weight, (((1,), (1,)), ((), ())), preferred_element_type=jnp.float32).astype(jnp.bfloat16)
        grad_prob = live * jnp.sum(grads.astype(jnp.float32) * proj, axis=1)
        partial_sum = lax.dot_general(rows, scaled, (((0,), (0,)), ((), ())), preferred_element_type=jnp.float32).astype(jnp.bfloat16)
        partial_sum = lax.optimization_barrier(partial_sum)
        return total + partial_sum.astype(jnp.float32), (output, grad_rows, grad_prob)

    start = jnp.zeros((FF, D), jnp.float32)
    total, (output, grad_hidden, grad_prob) = lax.scan(step, start, (hid_blocks, prob_blocks, cot_blocks, counts))
    return output.reshape(TOKENS, D), grad_hidden.reshape(TOKENS, FF), grad_prob.reshape(TOKENS), total
```

```python
import jax
import jax.numpy as jnp
from jax import lax
from jax.experimental import pallas as pl
from jax.experimental.pallas import tpu as pltpu
from jax.sharding import PartitionSpec as P

MESH = pl.DeviceIdType.MESH
F32, BF16 = jnp.float32, jnp.bfloat16
NX, NY, NZ, LO = 4, 8, 8, 4
ROWS, FF, D, SHARD = 384, 768, 2048, 12
SEMS = 144


def device(x, y, z, c):
    x, y, z, c = lax.rem(x, NX), lax.rem(y, NY), lax.rem(z, NZ), lax.rem(c, 2)
    return (lax.div(y, LO) * NX + x, z * (2 * LO) + lax.rem(y, LO) * 2 + c)


def kernel(
    hidden_h, prob_h, counts_s, weight_h, cot_h, out_h, gh_h, gp_h, gw_h,
    hid, hid_t, cot, scaled, prob, wgt, own_p, oth_p, rcv_p, ring, shard_in, shard, unit,
    blocks, full, out, gh_acc, gh, gp_acc, gp, send_z, recv_z, send_y, recv_y, recv_x, core_s, core_r, gw,
    local, ssem, rsem,
):
    r, s = lax.axis_index("rep"), lax.axis_index("shard")
    x, yh = lax.rem(r, NX), lax.div(r, NX)
    z, yl, c = lax.div(s, 2 * LO), lax.rem(lax.div(s, 2), LO), lax.rem(s, 2)
    y = yh * LO + yl
    px = lax.rem(x, 2)
    first = c == 0

    def at(dx=0, dy=0, dz=0, dc=0):
        return device(x + dx + NX, y + dy + NY, z + dz + NZ, c + dc)

    barrier = pltpu.get_barrier_semaphore()
    peers = [at(dc=1)] + [at(dx=k) for k in (1, 2, 3)]
    peers += [at(dy=k) for k in range(1, 8)] + [at(dz=k) for k in range(1, 8)]
    peers += [at(dy=4, dz=k) for k in range(1, 8)]
    for peer in peers:
        pl.semaphore_signal(barrier, inc=1, device_id=peer, device_id_type=MESH)

    loads = [
        pltpu.make_async_copy(a, b, local.at[i])
        for i, (a, b) in enumerate([(prob_h, prob), (hidden_h, hid), (cot_h, cot), (weight_h, shard_in)])
    ]
    for load in loads:
        load.start()

    used, sent = [0], []

    def group(n):
        used[0] += n
        assert used[0] <= SEMS
        return used[0] - n

    def push(src, dst, ssem_i, rsem_i, to):
        copy = pltpu.make_async_remote_copy(
            src, dst, ssem.at[ssem_i], rsem.at[rsem_i], device_id=to, device_id_type=MESH
        )
        copy.start()
        sent.append(copy)

    def arrive(dst, rsem_i):
        pltpu.make_async_remote_copy(
            dst, dst, ssem.at[0], rsem.at[rsem_i], device_id=at(dc=1), device_id_type=MESH
        ).wait_recv()

    loads[0].wait()
    place = lax.broadcasted_iota(jnp.int32, (1, ROWS), 1)
    live_row = (place < counts_s[0]).astype(F32)
    row = prob[...] * live_row
    wgt[...] = jnp.broadcast_to(row, (128, ROWS)).T
    loads[1].wait()
    hid_t[...] = hid[...].T
    loads[2].wait()
    for k in range(D // 128):
        at_k = pl.ds(128 * k, 128)
        scaled[:, at_k] = (wgt[...] * cot[:, at_k].astype(F32)).astype(BF16)
    loads[3].wait()
    shard[0] = jnp.concatenate([shard_in[...].astype(F32), jnp.zeros((4, D), F32)], axis=0).astype(BF16)

    for half, keep in ((1 - c, oth_p), (c, own_p)):
        for n in range(4):
            cols = pl.ds(pl.multiple_of(half * (D // 2) + 256 * n, 256), 256)
            part = jnp.dot(hid_t[...], scaled[:, cols], preferred_element_type=F32)
            if n < 2:
                keep[0, :, pl.ds(96 * n, 96), :] = part.astype(BF16).reshape(8, 96, 256)
            else:
                split = part.reshape(8, 4, 24, 256)
                for k in range(4):
                    keep[1, 4 * (n - 2) + k] = split[:, k].reshape(192, 256).astype(BF16)

    pl.semaphore_wait(barrier, len(peers))

    g_shard = group(1)
    push(shard.at[0], shard.at[1], g_shard, g_shard, at(dc=1))
    place_of = (z, y)
    order = [4, 3, -3, 2, -2, 1, -1, 0]
    g_pair = group(16)
    for i, k in enumerate(order):
        for a in range(2):
            dest = lax.rem(place_of[a] + k + 8, 8)
            push(oth_p.at[a, dest], rcv_p.at[a, dest], g_pair + 2 * i + a, g_pair + 2 * i + a, at(dc=1))

    paired = set()

    def pair(a, k):
        i = order.index(k)
        dest = lax.rem(place_of[a] + k + 8, 8)
        if (a, k) not in paired:
            paired.add((a, k))
            arrive(rcv_p.at[a, dest], g_pair + 2 * i + a)
        return dest

    g_ring = group(32)

    def slot(a, d, sub, t):
        return ((a * 2 + d) * 2 + sub) * 4 + t - 1

    def ring_step(t):
        for a in range(2):
            for d in range(2):
                for sub in ((0, 1) if d == 0 else (1, 0)):
                    if t == 1 and sub != d:
                        continue
                    k = (5 - t) * (1 if d == 0 else -1)
                    dest = pair(a, 4 if k == -4 else k)
                    rows = pl.ds(96 * sub, 96)
                    total = own_p[a, dest, rows, :].astype(F32) + rcv_p[a, dest, rows, :].astype(F32)
                    if t > 2 or (t == 2 and sub == d):
                        m = slot(a, d, sub, t - 1)
                        arrive(ring.at[m], g_ring + m)
                        total = total + ring[m].astype(F32)
                    own_p[a, dest, rows, :] = total.astype(BF16)
                    m = slot(a, d, sub, t)
                    step = 1 if d == 0 else -1
                    push(own_p.at[a, dest, rows, :], ring.at[m], g_ring + m, g_ring + m,
                         at(dz=step) if a == 0 else at(dy=step))

    def ring_end(a):
        dest = pair(a, 0)
        ends = []
        for sub in range(2):
            rows = pl.ds(96 * sub, 96)
            total = own_p[a, dest, rows, :].astype(F32) + rcv_p[a, dest, rows, :].astype(F32)
            for d in range(2):
                m = slot(a, d, sub, 4)
                arrive(ring.at[m], g_ring + m)
                total = total + ring[m].astype(F32)
            ends.append(total)
        return ends

    ring_step(1)

    q = c * 2 + px
    arrive(shard.at[1], g_shard)
    cols = pl.ds(pl.multiple_of(q * 512, 512), 512)
    mine, others = shard[0, :, cols].astype(F32)[:SHARD], shard[1, :, cols].astype(F32)[:SHARD]
    unit[0:SHARD, :] = jnp.where(first, mine, others)
    unit[SHARD : 2 * SHARD, :] = jnp.where(first, others, mine)
    u = unit[...]
    blocks[q, yl, z] = jnp.concatenate([u[:, :256], u[:, 256:]], axis=0).astype(BF16)
    g_wz = group(8)
    g_wz_s = group(7)
    for i, k in enumerate((4, 3, -3, 2, -2, 1, -1)):
        push(blocks.at[q, yl, z], blocks.at[q, yl, z], g_wz_s + i, g_wz + z, at(dz=k))

    ring_step(2)

    for k in range(1, 8):
        zk = lax.rem(z + k, 8)
        arrive(blocks.at[q, yl, zk], g_wz + zk)
    g_wy = group(4)
    low, high = pl.ds(0, 4), pl.ds(4, 4)
    push(blocks.at[q, yl], blocks.at[q, yl], g_wy, g_wy, at(dy=1))
    push(blocks.at[q, yl], blocks.at[q, yl], g_wy + 1, g_wy + 1, at(dy=-1))
    push(blocks.at[q, yl, low], blocks.at[q, yl, low], g_wy + 2, g_wy + 2, at(dy=2))
    push(blocks.at[q, yl, high], blocks.at[q, yl, high], g_wy + 3, g_wy + 3, at(dy=-2))

    g_wx, g_wc, g_wd = group(8), group(4), group(4)
    yls = [yl, lax.rem(yl + 3, 4), lax.rem(yl + 1, 4), lax.rem(yl + 2, 4)]

    def spread(j):
        ylj = yls[j]
        push(blocks.at[q, ylj, low], blocks.at[q, ylj, low], g_wx + j, g_wx + j, at(dx=1))
        push(blocks.at[q, ylj, high], blocks.at[q, ylj, high], g_wx + 4 + j, g_wx + 4 + j, at(dx=-1))
        push(blocks.at[q, ylj], blocks.at[q, ylj], g_wc + j, g_wc + j, at(dc=1))

    q2 = c * 2 + 1 - px

    def relay(j):
        ylj = yls[j]
        arrive(blocks.at[q2, ylj, low], g_wx + j)
        arrive(blocks.at[q2, ylj, high], g_wx + 4 + j)
        push(blocks.at[q2, ylj], blocks.at[q2, ylj], g_wd + j, g_wd + j, at(dc=1))

    spread(0)
    ring_step(3)
    ring_step(4)
    arrive(blocks.at[q, yls[1]], g_wy)
    spread(1)
    arrive(blocks.at[q, yls[2]], g_wy + 1)
    spread(2)

    ends = ring_end(0)
    for k in range(4):
        rows = slice(24 * k, 24 * k + 24)
        send_z[k] = jnp.concatenate([ends[0][rows], ends[1][rows]], axis=0).astype(BF16)
    g_z = group(8)
    g_z_s = group(7)
    for i, k in enumerate((4, 3, -3, 2, -2, 1, -1)):
        to = lax.rem(yl + k + 4, 4)
        push(send_z.at[to], recv_z.at[y], g_z_s + i, g_z + y, at(dy=k))
    recv_z[y] = send_z[yl]
    ends = ring_end(1)
    for k in range(8):
        block = ends[k // 4][24 * (k % 4) : 24 * (k % 4) + 24]
        send_y[k] = jnp.concatenate([block[:, :128], block[:, 128:]], axis=0).astype(BF16)
    g_y = group(16)
    g_y_s = group(15)
    me = yh * 8 + z
    for i, k in enumerate((4, 3, -3, 2, -2, 1, -1, 0)):
        to = lax.rem(z + k + 8, 8)
        push(send_y.at[to], recv_y.at[me], g_y_s + 2 * i, g_y + me, at(dy=4, dz=k))
        if k:
            push(send_y.at[to], recv_y.at[me], g_y_s + 2 * i + 1, g_y + me, at(dz=k))
    recv_y[me] = send_y[z]

    arrive(blocks.at[q, yls[3], low], g_wy + 2)
    arrive(blocks.at[q, yls[3], high], g_wy + 3)
    spread(3)

    def assemble(i, qi):
        for zi in range(8):
            for h in range(2):
                rows = [blocks[qi, k, zi, pl.ds(0, 48), :].astype(F32)[24 * h : 24 * h + 24] for k in range(4)]
                full[i, pl.ds(96 * zi, 96), pl.ds(256 * h, 256)] = jnp.concatenate(rows, axis=0).astype(BF16)

    stores = []

    def multiply(i, qi, start):
        cols = pl.ds(pl.multiple_of(qi * 512, 512), 512)
        proj = jnp.dot(hid[...], full[i], preferred_element_type=F32)
        for k in range(4):
            p = proj[:, 128 * k : 128 * k + 128]
            at_k = pl.ds(pl.multiple_of(qi * 512 + 128 * k, 128), 128)
            out[:, at_k] = (wgt[...] * p).astype(BF16)
            term = cot[:, at_k].astype(F32) * p
            gp_acc[...] = term if start and k == 0 else gp_acc[...] + term
        copy = pltpu.make_async_copy(out.at[:, cols], out_h.at[:, cols], local.at[4 + i])
        copy.start()
        stores.append(copy)
        back = lax.dot_general(scaled[:, cols], full[i], (((1,), (1,)), ((), ())), preferred_element_type=F32)
        gh_acc[...] = back if start else gh_acc[...] + back

    assemble(0, q)
    multiply(0, q, True)

    for k in range(1, 8):
        yk = lax.rem(y + k, 8)
        arrive(recv_z.at[yk], g_z + yk)
    total_z = recv_z[0].astype(F32)
    for k in range(1, 8):
        total_z = total_z + recv_z[k].astype(F32)
    for k in range(1, 16):
        mk = lax.rem(me + k, 16)
        arrive(recv_y.at[mk], g_y + mk)
    total_y = []
    for h in range(2):
        total = recv_y[8 * h].astype(F32)
        for k in range(1, 8):
            total = total + recv_y[8 * h + k].astype(F32)
        total_y.append(total)
    recv_x[x] = jnp.concatenate([total_z, jnp.concatenate(total_y, axis=1)], axis=0).astype(BF16)
    g_x = group(4)
    g_x_s = group(3)
    for i, k in enumerate((2, 1, 3)):
        push(recv_x.at[x], recv_x.at[x], g_x_s + i, g_x + x, at(dx=k))

    for j in range(3):
        relay(j)

    q3 = (1 - c) * 2 + px
    for j in range(4):
        arrive(blocks.at[q3, yls[j]], g_wc + j)
    assemble(1, q3)
    multiply(1, q3, False)
    relay(3)

    for k in range(1, 4):
        xk = lax.rem(x + k, 4)
        arrive(recv_x.at[xk], g_x + xk)
    total = recv_x[0].astype(F32)
    for k in range(1, 4):
        total = total + recv_x[k].astype(F32)
    core_s[...] = total
    g_core = group(1)
    push(core_s, core_r, g_core, g_core, at(dc=1))

    assemble(2, q2)
    multiply(2, q2, False)

    arrive(core_r, g_core)
    for h in range(2):
        f = jnp.where(first, core_s[...], core_r[...]) if h == 0 else jnp.where(first, core_r[...], core_s[...])
        parts = [f[0:24], f[24:48], f[48:72, :128], f[72:96, :128], f[48:72, 128:], f[72:96, 128:]]
        offset = h * (D // 2)
        for part in parts:
            width = part.shape[1]
            gw[:, pl.ds(offset, width)] = jnp.where(first, part[0:SHARD], part[SHARD:])
            offset += width
    copy = pltpu.make_async_copy(gw, gw_h, local.at[8])
    copy.start()
    stores.append(copy)

    q4 = (1 - c) * 2 + 1 - px
    for j in range(4):
        arrive(blocks.at[q4, yls[j]], g_wd + j)
    assemble(3, q4)
    multiply(3, q4, False)
    gh[...] = gh_acc[...].astype(BF16)
    copy = pltpu.make_async_copy(gh, gh_h, local.at[9])
    copy.start()
    stores.append(copy)
    gp[...] = live_row * jnp.sum(gp_acc[...].T, axis=0, keepdims=True)
    copy = pltpu.make_async_copy(gp, gp_h, local.at[10])
    copy.start()
    stores.append(copy)

    for copy in stores:
        copy.wait()
    for copy in sent:
        copy.wait_send()


def body(hidden, prob, counts, down_weight, cotangent):
    hbm = pl.BlockSpec(memory_space=pl.ANY)
    vmem = pltpu.VMEM
    output, grad_hidden, grad_prob, grad_weight = pl.pallas_call(
        kernel,
        name="expert_down",
        out_shape=(
            jax.ShapeDtypeStruct((ROWS, D), BF16),
            jax.ShapeDtypeStruct((ROWS, FF), BF16),
            jax.ShapeDtypeStruct((1, ROWS), F32),
            jax.ShapeDtypeStruct((SHARD, D), F32),
        ),
        in_specs=[hbm, hbm, pl.BlockSpec(memory_space=pltpu.SMEM), hbm, hbm],
        out_specs=(hbm, hbm, hbm, hbm),
        scratch_shapes=[
            vmem((ROWS, FF), BF16),
            vmem((FF, ROWS), BF16),
            vmem((ROWS, D), BF16),
            vmem((ROWS, D), BF16),
            vmem((1, ROWS), F32),
            vmem((ROWS, 128), F32),
            vmem((2, 8, 192, 256), BF16),
            vmem((2, 8, 192, 256), BF16),
            vmem((2, 8, 192, 256), BF16),
            vmem((32, 96, 256), BF16),
            vmem((SHARD, D), BF16),
            vmem((2, 16, D), BF16),
            vmem((2 * SHARD, 512), F32),
            vmem((4, 4, 8, 48, 256), BF16),
            vmem((4, FF, 512), BF16),
            vmem((ROWS, D), BF16),
            vmem((ROWS, FF), F32),
            vmem((ROWS, FF), BF16),
            vmem((ROWS, 128), F32),
            vmem((1, ROWS), F32),
            vmem((4, 48, 256), BF16),
            vmem((8, 48, 256), BF16),
            vmem((8, 48, 128), BF16),
            vmem((16, 48, 128), BF16),
            vmem((4, 96, 256), BF16),
            vmem((96, 256), F32),
            vmem((96, 256), F32),
            vmem((SHARD, D), F32),
            pltpu.SemaphoreType.DMA((11,)),
            pltpu.SemaphoreType.DMA((SEMS,)),
            pltpu.SemaphoreType.DMA((SEMS,)),
        ],
        compiler_params=pltpu.CompilerParams(
            collective_id=0, has_side_effects=True, vmem_limit_bytes=48 * 2**20
        ),
    )(hidden, prob.reshape(1, ROWS), counts, down_weight, cotangent)
    return output, grad_hidden, grad_prob.reshape(ROWS), grad_weight


def solution(mesh):
    placed = (
        P(("rep", "shard"), None),
        P(("rep", "shard")),
        P(("rep", "shard")),
        P("shard", None),
        P(("rep", "shard"), None),
    )
    return jax.shard_map(
        body,
        mesh=mesh,
        in_specs=placed,
        out_specs=(
            P(("rep", "shard"), None),
            P(("rep", "shard"), None),
            P(("rep", "shard")),
            P("shard", None),
        ),
        check_vma=False,
    )
```

```python
import jax
import jax.numpy as jnp
from jax import lax
from jax.experimental import pallas as pl
from jax.experimental.pallas import tpu as pltpu
from jax.sharding import PartitionSpec as P

AG, RS = True, True
MESH = pl.DeviceIdType.MESH
F32, BF16 = jnp.float32, jnp.bfloat16
NX, NY, NZ, LO = 4, 8, 8, 4
ROWS, FF, D, SHARD = 384, 768, 2048, 12
SEMS = 192


def device(x, y, z, c):
    x, y, z, c = lax.rem(x, NX), lax.rem(y, NY), lax.rem(z, NZ), lax.rem(c, 2)
    return (lax.div(y, LO) * NX + x, z * (2 * LO) + lax.rem(y, LO) * 2 + c)


def kernel(
    hidden_h, prob_h, counts_s, weight_h, cot_h, out_h, gh_h, gp_h, gw_h,
    hid, hid_t, cot, scaled, prob, wgt, own_z, own_x, oth_z, oth_x, rcv_z, rcv_x, ring_z, ring_x, shard_in, shard, unit,
    blocks, full, out, gh_acc, gh, gp_acc, gp, send_z, recv_z, send_yz, recv_yz, send_yx, recv_yx, recv_x, core_s, core_r, gw,
    local, ssem, rsem,
):
    r, s = lax.axis_index("rep"), lax.axis_index("shard")
    x, yh = lax.rem(r, NX), lax.div(r, NX)
    z, yl, c = lax.div(s, 2 * LO), lax.rem(lax.div(s, 2), LO), lax.rem(s, 2)
    y = yh * LO + yl
    first = c == 0

    def at(dx=0, dy=0, dz=0, dc=0):
        return device(x + dx + NX, y + dy + NY, z + dz + NZ, c + dc)

    barrier = pltpu.get_barrier_semaphore()
    peers = [at(dc=1)] + [at(dx=k) for k in (1, 2, 3)]
    peers += [at(dy=k) for k in range(1, 8)] + [at(dz=k) for k in range(1, 8)]
    for peer in peers:
        pl.semaphore_signal(barrier, inc=1, device_id=peer, device_id_type=MESH)

    loads = [
        pltpu.make_async_copy(a, b, local.at[i])
        for i, (a, b) in enumerate([(prob_h, prob), (hidden_h, hid), (weight_h, shard_in)])
    ]
    for load in loads:
        load.start()
    cot_loads = []
    for i, half in enumerate((1 - c, c)):
        cols = pl.ds(pl.multiple_of(half * (D // 2), D // 2), D // 2)
        load = pltpu.make_async_copy(cot_h.at[:, cols], cot.at[:, cols], local.at[3 + i])
        load.start()
        cot_loads.append(load)

    used, sent = [0], []

    def group(n):
        used[0] += n
        assert used[0] <= SEMS
        return used[0] - n

    def push(src, dst, ssem_i, rsem_i, to):
        copy = pltpu.make_async_remote_copy(
            src, dst, ssem.at[ssem_i], rsem.at[rsem_i], device_id=to, device_id_type=MESH
        )
        copy.start()
        sent.append(copy)

    def arrive(dst, rsem_i):
        pltpu.make_async_remote_copy(
            dst, dst, ssem.at[0], rsem.at[rsem_i], device_id=at(dc=1), device_id_type=MESH
        ).wait_recv()

    loads[0].wait()
    place = lax.broadcasted_iota(jnp.int32, (1, ROWS), 1)
    live_row = (place < counts_s[0]).astype(F32)
    row = prob[...].reshape(1, ROWS) * live_row
    wgt[...] = jnp.broadcast_to(row, (128, ROWS)).T
    loads[1].wait()
    hid_t[...] = hid[...].T

    def partials(half, keep_z, keep_x, ns):
        for n in ns:
            start = half * (D // 2) + 256 * n
            for k in range(2):
                at_k = pl.ds(pl.multiple_of(start + 128 * k, 128), 128)
                scaled[:, at_k] = (wgt[...] * cot[:, at_k].astype(F32)).astype(BF16)
            cols = pl.ds(pl.multiple_of(start, 256), 256)
            part = jnp.dot(hid_t[...], scaled[:, cols], preferred_element_type=F32)
            if n < 2:
                keep_z[:, pl.ds(96 * n, 96), :] = part.astype(BF16).reshape(8, 96, 256)
            else:
                for k in range(2):
                    keep_x[2 * (n - 2) + k] = part[:, 128 * k : 128 * k + 128].astype(BF16)

    orders = ([4, 3, -3, 2, -2, 1, -1, 0], [2, 1, -1, 0])
    place_of, length = (z, x), (NZ, NX)
    own, oth, rcv = (own_z, own_x), (oth_z, oth_x), (rcv_z, rcv_x)
    g_shard, g_pair = group(1), (group(8), group(4))

    def push_pair(a):
        for i, k in enumerate(orders[a] if RS else []):
            dest = lax.rem(place_of[a] + k + length[a], length[a])
            push(oth[a].at[dest], rcv[a].at[dest], g_pair[a] + i, g_pair[a] + i, at(dc=1))

    cot_loads[0].wait()
    partials(1 - c, oth_z, oth_x, (0, 1))
    loads[2].wait()
    shard[0] = jnp.concatenate([shard_in[...].astype(F32), jnp.zeros((4, D), F32)], axis=0).astype(BF16)
    def rs(f, *args):
        return f(*args) if RS else None

    def ag(f, *args):
        return f(*args) if AG else None

    qs = [c * 4 + lax.rem(x + k, 4) for k in range(4)] + [(1 - c) * 4 + lax.rem(x + k, 4) for k in range(4)]
    yls = [yl, lax.rem(yl + 3, 4), lax.rem(yl + 1, 4), lax.rem(yl + 2, 4)]
    low, high = pl.ds(0, 4), pl.ds(4, 4)
    g_wz, g_wz_s, g_wy, g_wx, g_wc = group(8), group(7), group(4), group(16), group(16)

    def make_unit():
        q = qs[0]
        arrive(shard.at[1], g_shard)
        cols = pl.ds(pl.multiple_of(q * 256, 256), 256)
        mine, others = shard[0, :, cols].astype(F32)[:SHARD], shard[1, :, cols].astype(F32)[:SHARD]
        unit[0:SHARD, :] = jnp.where(first, mine, others)
        unit[SHARD : 2 * SHARD, :] = jnp.where(first, others, mine)
        u = unit[...]
        blocks[q, yl, z] = jnp.concatenate([u[:, :128], u[:, 128:]], axis=0).astype(BF16)
        for i, k in enumerate((4, 3, -3, 2, -2, 1, -1)):
            push(blocks.at[q, yl, z], blocks.at[q, yl, z], g_wz_s + i, g_wz + z, at(dz=k))

    def along_y():
        q = qs[0]
        for k in range(1, 8):
            zk = lax.rem(z + k, 8)
            arrive(blocks.at[q, yl, zk], g_wz + zk)
        push(blocks.at[q, yl], blocks.at[q, yl], g_wy, g_wy, at(dy=1))
        push(blocks.at[q, yl], blocks.at[q, yl], g_wy + 1, g_wy + 1, at(dy=-1))
        push(blocks.at[q, yl, low], blocks.at[q, yl, low], g_wy + 2, g_wy + 2, at(dy=2))
        push(blocks.at[q, yl, high], blocks.at[q, yl, high], g_wy + 3, g_wy + 3, at(dy=-2))

    pl.semaphore_wait(barrier, len(peers))
    if AG:
        push(shard.at[0], shard.at[1], g_shard, g_shard, at(dc=1))
    push_pair(0)
    partials(1 - c, oth_z, oth_x, (2, 3))
    push_pair(1)
    if AG:
        make_unit()
    cot_loads[1].wait()
    partials(c, own_z, own_x, (0, 1, 2, 3))

    paired = set()

    def pair(a, k):
        k = length[a] // 2 if k == -length[a] // 2 else k
        dest = lax.rem(place_of[a] + k + length[a], length[a])
        if (a, k) not in paired:
            paired.add((a, k))
            arrive(rcv[a].at[dest], g_pair[a] + orders[a].index(k))
        return dest

    rings, height = (ring_z, ring_x), (48, 192)
    g_ring = (group(32), group(16))

    def slot(a, d, sub, t):
        return ((d * 4) + sub) * (length[a] // 2) + t - 1

    def ring_step(a, t):
        for i in range(2 if t == 1 else 4):
            for d in range(2):
                far = t == 1 or i >= 2
                sub = (i % 2) + 2 * (d if far else 1 - d)
                dest = pair(a, (length[a] // 2 + 1 - t) * (1 if d == 0 else -1))
                rows = pl.ds(height[a] * sub, height[a])
                total = own[a][dest, rows, :].astype(F32) + rcv[a][dest, rows, :].astype(F32)
                if t > 2 or (t == 2 and far):
                    m = slot(a, d, sub, t - 1)
                    arrive(rings[a].at[m], g_ring[a] + m)
                    total = total + rings[a][m].astype(F32)
                own[a][dest, rows, :] = total.astype(BF16)
                m = slot(a, d, sub, t)
                step = 1 if d == 0 else -1
                push(own[a].at[dest, rows, :], rings[a].at[m], g_ring[a] + m, g_ring[a] + m,
                     at(dz=step) if a == 0 else at(dx=step))

    def ring_end(a):
        dest = pair(a, 0)
        ends = []
        for sub in range(4):
            rows = pl.ds(height[a] * sub, height[a])
            ends.append(own[a][dest, rows, :].astype(F32) + rcv[a][dest, rows, :].astype(F32))
        for i in range(4):
            for d in range(2):
                sub = (i % 2) + 2 * (1 - d if i < 2 else d)
                m = slot(a, d, sub, length[a] // 2)
                arrive(rings[a].at[m], g_ring[a] + m)
                ends[sub] = ends[sub] + rings[a][m].astype(F32)
        return ends

    def to_core(k, j):
        block = blocks.at[qs[k], yls[j]]
        push(block, block, g_wc + 4 * k + j, g_wc + 4 * k + j, at(dc=1))

    def spread(j):
        if j in (1, 2):
            arrive(blocks.at[qs[0], yls[j]], g_wy + j - 1)
        if j == 3:
            arrive(blocks.at[qs[0], yls[3], low], g_wy + 2)
            arrive(blocks.at[qs[0], yls[3], high], g_wy + 3)
        block = blocks.at[qs[0], yls[j]]
        push(block, block, g_wx + j, g_wx + j, at(dx=1))
        push(block, block, g_wx + 4 + j, g_wx + 4 + j, at(dx=-1))
        to_core(0, j)

    def forward(j):
        arrive(blocks.at[qs[3], yls[j]], g_wx + j)
        part = blocks.at[qs[3], yls[j], low]
        push(part, part, g_wx + 8 + j, g_wx + 8 + j, at(dx=1))
        arrive(blocks.at[qs[1], yls[j]], g_wx + 4 + j)
        part = blocks.at[qs[1], yls[j], high]
        push(part, part, g_wx + 12 + j, g_wx + 12 + j, at(dx=-1))
        to_core(3, j)
        to_core(1, j)

    def last(j):
        arrive(blocks.at[qs[2], yls[j], low], g_wx + 8 + j)
        arrive(blocks.at[qs[2], yls[j], high], g_wx + 12 + j)
        to_core(2, j)

    stores = []

    def multiply(i):
        if i >= 4:
            for j in range(4):
                arrive(blocks.at[qs[i], yls[j]], g_wc + 4 * (i - 4) + j)
        qi = qs[i]
        for zi in range(8):
            for h in range(2):
                rows = [blocks[qi, k, zi].astype(F32)[24 * h : 24 * h + 24] for k in range(4)]
                full[i, pl.ds(96 * zi, 96), pl.ds(128 * h, 128)] = jnp.concatenate(rows, axis=0).astype(BF16)
        cols = pl.ds(pl.multiple_of(qi * 256, 256), 256)
        proj = jnp.dot(hid[...], full[i], preferred_element_type=F32)
        for k in range(2):
            p = proj[:, 128 * k : 128 * k + 128]
            at_k = pl.ds(pl.multiple_of(qi * 256 + 128 * k, 128), 128)
            out[:, at_k] = (wgt[...] * p).astype(BF16)
            term = cot[:, at_k].astype(F32) * p
            gp_acc[...] = term if not stores and k == 0 else gp_acc[...] + term
        back = lax.dot_general(scaled[:, cols], full[i], (((1,), (1,)), ((), ())), preferred_element_type=F32)
        gh_acc[...] = back if not stores else gh_acc[...] + back
        copy = pltpu.make_async_copy(out.at[:, cols], out_h.at[:, cols], local.at[5 + i])
        copy.start()
        stores.append(copy)

    far_first = (4, 3, -3, 2, -2, 1, -1)
    g_z, g_z_s, g_yz, g_yz_s, g_yx, g_yx_s = group(8), group(7), group(8), group(7), group(8), group(7)
    g_x, g_x_s, g_core = group(4), group(3), group(1)
    none = jnp.zeros((8, 128), F32)

    def across_z():
        ends = ring_end(1)
        for k in range(8):
            send_z[k] = ends[k // 2][96 * (k % 2) : 96 * (k % 2) + 96].astype(BF16)
        for i, k in enumerate(far_first):
            to = lax.rem(z + k + 8, 8)
            push(send_z.at[to], recv_z.at[z], g_z_s + i, g_z + z, at(dz=k))
        recv_z[z] = send_z[z]

    def across_y(send, recv, base, base_s):
        for i, k in enumerate(far_first):
            to = lax.rem(yl + k + 4, 4)
            push(send.at[to], recv.at[y], base_s + i, base + y, at(dy=k))
        recv[y] = send[yl]

    def across_y_z():
        ends = ring_end(0)
        for k in range(4):
            rows = slice(24 * (k % 2), 24 * (k % 2) + 24)
            low_cols, high_cols = ends[k // 2][rows], ends[2 + k // 2][rows]
            parts = [low_cols[:, :128], low_cols[:, 128:], high_cols[:, :128], high_cols[:, 128:]]
            send_yz[k] = jnp.concatenate(parts, axis=0).astype(BF16)
        across_y(send_yz, recv_yz, g_yz, g_yz_s)

    def gathered(recv, base, mine, n):
        for k in range(1, n):
            at_k = lax.rem(mine + k, n)
            arrive(recv.at[at_k], base + at_k)
        total = recv[0].astype(F32)
        for k in range(1, n):
            total = total + recv[k].astype(F32)
        return total

    def across_y_x():
        total = gathered(recv_z, g_z, z, 8)
        for k in range(4):
            send_yx[k] = jnp.concatenate([total[24 * k : 24 * k + 24], none], axis=0).astype(BF16)
        across_y(send_yx, recv_yx, g_yx, g_yx_s)

    def exchange_x():
        total_z = gathered(recv_yz, g_yz, y, 8)
        total_x = gathered(recv_yx, g_yx, y, 8)
        recv_x[x] = jnp.concatenate([total_z, total_x], axis=0).astype(BF16)
        for i, k in enumerate((2, 1, 3)):
            push(recv_x.at[x], recv_x.at[x], g_x_s + i, g_x + x, at(dx=k))

    def exchange_core():
        total = gathered(recv_x, g_x, x, 4)
        core_s[pl.ds(0, 96), :] = total[:96]
        for k in range(4):
            core_s[pl.ds(96 + 24 * k, 24), :] = recv_x[k].astype(F32)[96:120]
        push(core_s, core_r, g_core, g_core, at(dc=1))

    def finish_sum():
        arrive(core_r, g_core)
        for h in range(2):
            f = jnp.where(first, core_s[...], core_r[...]) if h == 0 else jnp.where(first, core_r[...], core_s[...])
            for k in range(8):
                part = f[24 * k : 24 * k + 24]
                gw[:, pl.ds(h * (D // 2) + 128 * k, 128)] = jnp.where(first, part[:SHARD], part[SHARD:])
        copy = pltpu.make_async_copy(gw, gw_h, local.at[13])
        copy.start()
        stores.append(copy)

    rs(ring_step, 0, 1)
    rs(ring_step, 1, 1)
    rs(ring_step, 1, 2)
    rs(ring_step, 0, 2)
    ag(along_y)
    ag(spread, 0)
    rs(ring_step, 0, 3)
    rs(ring_step, 0, 4)
    rs(across_z)
    ag(spread, 1)
    ag(spread, 2)
    ag(forward, 0)
    rs(across_y_z)
    ag(spread, 3)
    rs(across_y_x)
    ag(multiply, 0)
    ag(forward, 1)
    ag(forward, 2)
    ag(multiply, 4)
    rs(exchange_x)
    ag(forward, 3)
    for j in range(3):
        ag(last, j)
    ag(multiply, 1)
    ag(multiply, 3)
    rs(exchange_core)
    ag(last, 3)
    ag(multiply, 5)
    rs(finish_sum)
    ag(multiply, 7)
    ag(multiply, 2)
    ag(multiply, 6)
    gh[...] = gh_acc[...].astype(BF16)
    copy = pltpu.make_async_copy(gh, gh_h, local.at[13])
    copy.start()
    stores.append(copy)
    gp[...] = (live_row * jnp.sum(gp_acc[...].T, axis=0, keepdims=True)).reshape(ROWS)
    copy = pltpu.make_async_copy(gp, gp_h, local.at[14])
    copy.start()
    stores.append(copy)

    for copy in stores:
        copy.wait()
    for copy in sent:
        copy.wait_send()


def pin(a):
    return pltpu.with_memory_space_constraint(a, pltpu.HBM)


def body(hidden, prob, counts, down_weight, cotangent):
    hbm = pl.BlockSpec(memory_space=pltpu.HBM)
    free = pl.BlockSpec(memory_space=pl.ANY)
    vmem = pltpu.VMEM
    output, grad_hidden, grad_prob, grad_weight = pl.pallas_call(
        kernel,
        name="expert_down",
        out_shape=(
            jax.ShapeDtypeStruct((ROWS, D), BF16),
            jax.ShapeDtypeStruct((ROWS, FF), BF16),
            jax.ShapeDtypeStruct((ROWS,), F32),
            jax.ShapeDtypeStruct((SHARD, D), F32),
        ),
        in_specs=[hbm, hbm, pl.BlockSpec(memory_space=pltpu.SMEM), hbm, hbm],
        out_specs=(free, free, free, free),
        scratch_shapes=[
            vmem((ROWS, FF), BF16),
            vmem((FF, ROWS), BF16),
            vmem((ROWS, D), BF16),
            vmem((ROWS, D), BF16),
            vmem((ROWS,), F32),
            vmem((ROWS, 128), F32),
            vmem((8, 192, 256), BF16),
            vmem((4, FF, 128), BF16),
            vmem((8, 192, 256), BF16),
            vmem((4, FF, 128), BF16),
            vmem((8, 192, 256), BF16),
            vmem((4, FF, 128), BF16),
            vmem((32, 48, 256), BF16),
            vmem((16, 192, 128), BF16),
            vmem((SHARD, D), BF16),
            vmem((2, 16, D), BF16),
            vmem((2 * SHARD, 256), F32),
            vmem((8, 4, 8, 48, 128), BF16),
            vmem((8, FF, 256), BF16),
            vmem((ROWS, D), BF16),
            vmem((ROWS, FF), F32),
            vmem((ROWS, FF), BF16),
            vmem((ROWS, 128), F32),
            vmem((ROWS,), F32),
            vmem((8, 96, 128), BF16),
            vmem((8, 96, 128), BF16),
            vmem((4, 96, 128), BF16),
            vmem((8, 96, 128), BF16),
            vmem((4, 32, 128), BF16),
            vmem((8, 32, 128), BF16),
            vmem((4, 128, 128), BF16),
            vmem((192, 128), F32),
            vmem((192, 128), F32),
            vmem((SHARD, D), F32),
            pltpu.SemaphoreType.DMA((16,)),
            pltpu.SemaphoreType.DMA((SEMS,)),
            pltpu.SemaphoreType.DMA((SEMS,)),
        ],
        compiler_params=pltpu.CompilerParams(
            collective_id=0, has_side_effects=True, vmem_limit_bytes=40 * 2**20
        ),
    )(pin(hidden), pin(prob), counts, pin(down_weight), pin(cotangent))
    return output, grad_hidden, grad_prob, grad_weight


def solution(mesh):
    placed = (
        P(("rep", "shard"), None),
        P(("rep", "shard")),
        P(("rep", "shard")),
        P("shard", None),
        P(("rep", "shard"), None),
    )
    return jax.shard_map(
        body,
        mesh=mesh,
        in_specs=placed,
        out_specs=(
            P(("rep", "shard"), None),
            P(("rep", "shard"), None),
            P(("rep", "shard")),
            P("shard", None),
        ),
        check_vma=False,
    )
```

```python
import jax
import jax.numpy as jnp
from jax import lax
from jax.experimental import pallas as pl
from jax.experimental.pallas import tpu as pltpu
from jax.sharding import PartitionSpec as P

MESH = pl.DeviceIdType.MESH
F32, BF16 = jnp.float32, jnp.bfloat16
NX, NY, NZ, LO = 4, 8, 8, 4
ROWS, FF, D, SHARD = 384, 768, 2048, 12
SEMS, KINDS = 78, 15


def device(x, y, z, c):
    x, y, z, c = lax.rem(x, NX), lax.rem(y, NY), lax.rem(z, NZ), lax.rem(c, 2)
    return (lax.div(y, LO) * NX + x, z * (2 * LO) + lax.rem(y, LO) * 2 + c)


def kernel(
    hidden_h, prob_h, counts_s, weight_h, cot_h, out_h, gh_h, gp_h, gw_h,
    hid, hid_t, cot, scaled, prob, wgt, own_z, own_x, oth_z, oth_x, rcv_z, rcv_x, ring_z, ring_x, shard_in, shard, unit,
    blocks, full, out, gh_acc, gh, gp_acc, gp, send_z, recv_z, send_yz, recv_yz, send_yx, recv_yx, recv_x, core_s, core_r, gw,
    local, ssem, rsem,
):
    r, s = lax.axis_index("rep"), lax.axis_index("shard")
    x, yh = lax.rem(r, NX), lax.div(r, NX)
    z, yl, c = lax.div(s, 2 * LO), lax.rem(lax.div(s, 2), LO), lax.rem(s, 2)
    y = yh * LO + yl
    first = c == 0

    def at(dx=0, dy=0, dz=0, dc=0):
        return device(x + dx + NX, y + dy + NY, z + dz + NZ, c + dc)

    barrier = pltpu.get_barrier_semaphore()
    peers = [at(dc=1)] + [at(dx=k) for k in (1, 2, 3)]
    peers += [at(dy=k) for k in range(1, 8)] + [at(dz=k) for k in range(1, 8)]
    for peer in peers:
        pl.semaphore_signal(barrier, inc=1, device_id=peer, device_id_type=MESH)

    loads = [
        pltpu.make_async_copy(a, b, local.at[i])
        for i, (a, b) in enumerate([(prob_h, prob), (hidden_h, hid), (weight_h, shard_in)])
    ]
    for load in loads:
        load.start()
    cot_loads = []
    for i, half in enumerate((1 - c, c)):
        cols = pl.ds(pl.multiple_of(half * (D // 2), D // 2), D // 2)
        load = pltpu.make_async_copy(cot_h.at[:, cols], cot.at[:, cols], local.at[3 + i])
        load.start()
        cot_loads.append(load)

    used, sends = [0], []

    def group(n):
        used[0] += n
        assert used[0] <= SEMS
        return used[0] - n

    def kind(total):
        sends.append(total)
        return len(sends) - 1

    def push(src, dst, of, rsem_i, to):
        pltpu.make_async_remote_copy(
            src, dst, ssem.at[of], rsem.at[rsem_i], device_id=to, device_id_type=MESH
        ).start()

    def arrive(dst, rsem_i):
        pltpu.make_async_remote_copy(
            dst, dst, ssem.at[0], rsem.at[rsem_i], device_id=at(dc=1), device_id_type=MESH
        ).wait_recv()

    loads[0].wait()
    place = lax.broadcasted_iota(jnp.int32, (1, ROWS), 1)
    live_row = (place < counts_s[0]).astype(F32)
    row = prob[...].reshape(1, ROWS) * live_row
    wgt[...] = jnp.broadcast_to(row, (128, ROWS)).T
    loads[1].wait()
    hid_t[...] = hid[...].T

    def partials(half, keep_z, keep_x, ns):
        for n in ns:
            start = half * (D // 2) + 256 * n
            for k in range(2):
                at_k = pl.ds(pl.multiple_of(start + 128 * k, 128), 128)
                scaled[:, at_k] = (wgt[...] * cot[:, at_k].astype(F32)).astype(BF16)
            cols = pl.ds(pl.multiple_of(start, 256), 256)
            part = jnp.dot(hid_t[...], scaled[:, cols], preferred_element_type=F32)
            if n < 2:
                keep_z[:, pl.ds(96 * n, 96), :] = part.astype(BF16).reshape(8, 96, 256)
            else:
                for k in range(2):
                    keep_x[2 * (n - 2) + k] = part[:, 128 * k : 128 * k + 128].astype(BF16)

    orders = ([4, 3, -3, 2, -2, 1, -1, 0], [2, 1, -1, 0])
    place_of, length = (z, x), (NZ, NX)
    own, oth, rcv = (own_z, own_x), (oth_z, oth_x), (rcv_z, rcv_x)
    g_shard, g_pair = group(1), (group(8), group(4))
    s_shard, s_pair = kind(shard.at[1]), (kind(rcv_z), kind(rcv_x))

    def push_pair(a):
        for i, k in enumerate(orders[a]):
            dest = lax.rem(place_of[a] + k + length[a], length[a])
            push(oth[a].at[dest], rcv[a].at[dest], s_pair[a], g_pair[a] + i, at(dc=1))

    cot_loads[0].wait()
    partials(1 - c, oth_z, oth_x, (0, 1))
    loads[2].wait()
    shard[0] = jnp.concatenate([shard_in[...].astype(F32), jnp.zeros((4, D), F32)], axis=0).astype(BF16)
    qs = [c * 4 + lax.rem(x + k, 4) for k in range(4)] + [(1 - c) * 4 + lax.rem(x + k, 4) for k in range(4)]
    yls = [yl, lax.rem(yl + 3, 4), lax.rem(yl + 1, 4), lax.rem(yl + 2, 4)]
    low, high = pl.ds(0, 4), pl.ds(4, 4)
    g_wz, g_wy, g_wx, g_wf, g_wc = group(1), group(3), group(8), group(4), group(4)
    s_wz, s_wy, s_wx, s_wf, s_wc = [
        kind(t) for t in (blocks.at[0, 0, pl.ds(0, 7)], blocks.at[0, pl.ds(0, 3)], blocks.at[pl.ds(0, 2)], blocks.at[0], blocks.at[pl.ds(0, 4)])
    ]

    def make_unit():
        q = qs[0]
        arrive(shard.at[1], g_shard)
        cols = pl.ds(pl.multiple_of(q * 256, 256), 256)
        mine, others = shard[0, :, cols].astype(F32)[:SHARD], shard[1, :, cols].astype(F32)[:SHARD]
        unit[0:SHARD, :] = jnp.where(first, mine, others)
        unit[SHARD : 2 * SHARD, :] = jnp.where(first, others, mine)
        u = unit[...]
        blocks[q, yl, z] = jnp.concatenate([u[:, :128], u[:, 128:]], axis=0).astype(BF16)
        for k in (4, 3, -3, 2, -2, 1, -1):
            push(blocks.at[q, yl, z], blocks.at[q, yl, z], s_wz, g_wz, at(dz=k))

    def along_y():
        q = qs[0]
        arrive(blocks.at[q, yl, pl.ds(0, 7)], g_wz)
        push(blocks.at[q, yl], blocks.at[q, yl], s_wy, g_wy, at(dy=1))
        push(blocks.at[q, yl], blocks.at[q, yl], s_wy, g_wy + 1, at(dy=-1))
        push(blocks.at[q, yl, low], blocks.at[q, yl, low], s_wy, g_wy + 2, at(dy=2))
        push(blocks.at[q, yl, high], blocks.at[q, yl, high], s_wy, g_wy + 2, at(dy=-2))

    pl.semaphore_wait(barrier, len(peers))
    push(shard.at[0], shard.at[1], s_shard, g_shard, at(dc=1))
    push_pair(0)
    partials(1 - c, oth_z, oth_x, (2, 3))
    push_pair(1)

    paired = set()

    def pair(a, k):
        k = length[a] // 2 if k == -length[a] // 2 else k
        dest = lax.rem(place_of[a] + k + length[a], length[a])
        if (a, k) not in paired:
            paired.add((a, k))
            arrive(rcv[a].at[dest], g_pair[a] + orders[a].index(k))
        return dest

    rings, height = (ring_z, ring_x), (48, 192)
    g_ring = (group(28), group(12))
    s_ring = (kind(ring_z), kind(ring_x))

    def slot(a, d, i, t, far):
        return 2 * d + i if t == 1 else 4 + 8 * (t - 2) + 4 * far + 2 * d + i

    def ring_step(a, t, far):
        for i in range(2):
            for d in range(2):
                sub = i + 2 * (d if far else 1 - d)
                dest = pair(a, (length[a] // 2 + 1 - t) * (1 if d == 0 else -1))
                rows = pl.ds(height[a] * sub, height[a])
                total = own[a][dest, rows, :].astype(F32) + rcv[a][dest, rows, :].astype(F32)
                if t > 2 or (t == 2 and far):
                    m = slot(a, d, i, t - 1, far)
                    arrive(rings[a].at[m], g_ring[a] + m)
                    total = total + rings[a][m].astype(F32)
                own[a][dest, rows, :] = total.astype(BF16)
                m = slot(a, d, i, t, far)
                step = 1 if d == 0 else -1
                push(own[a].at[dest, rows, :], rings[a].at[m], s_ring[a], g_ring[a] + m,
                     at(dz=step) if a == 0 else at(dx=step))

    def ring_end(a):
        dest = pair(a, 0)
        ends = []
        for sub in range(4):
            rows = pl.ds(height[a] * sub, height[a])
            ends.append(own[a][dest, rows, :].astype(F32) + rcv[a][dest, rows, :].astype(F32))
        for far in (False, True):
            for i in range(2):
                for d in range(2):
                    sub = i + 2 * (d if far else 1 - d)
                    m = slot(a, d, i, length[a] // 2, far)
                    arrive(rings[a].at[m], g_ring[a] + m)
                    ends[sub] = ends[sub] + rings[a][m].astype(F32)
        return ends

    def to_core(k, j):
        block = blocks.at[qs[k], yls[j]]
        push(block, block, s_wc, g_wc + k, at(dc=1))

    def spread(j):
        if j in (1, 2):
            arrive(blocks.at[qs[0], yls[j]], g_wy + j - 1)
        if j == 3:
            arrive(blocks.at[qs[0], yls[3]], g_wy + 2)
        block = blocks.at[qs[0], yls[j]]
        push(block, block, s_wx, g_wx + j, at(dx=1))
        push(block, block, s_wx, g_wx + 4 + j, at(dx=-1))
        to_core(0, j)

    def forward(j):
        arrive(blocks.at[qs[3], yls[j]], g_wx + j)
        part = blocks.at[qs[3], yls[j], low]
        push(part, part, s_wf, g_wf + j, at(dx=1))
        arrive(blocks.at[qs[1], yls[j]], g_wx + 4 + j)
        part = blocks.at[qs[1], yls[j], high]
        push(part, part, s_wf, g_wf + j, at(dx=-1))
        to_core(3, j)
        to_core(1, j)

    def last(j):
        arrive(blocks.at[qs[2], yls[j]], g_wf + j)
        to_core(2, j)

    stores, done = [], []

    def multiply(i):
        if i >= 4:
            arrive(blocks.at[qs[i]], g_wc + i - 4)
        qi = qs[i]
        for zi in range(8):
            for h in range(2):
                rows = [blocks[qi, k, zi].astype(F32)[24 * h : 24 * h + 24] for k in range(4)]
                full[i, pl.ds(96 * zi, 96), pl.ds(128 * h, 128)] = jnp.concatenate(rows, axis=0).astype(BF16)
        cols = pl.ds(pl.multiple_of(qi * 256, 256), 256)
        proj = jnp.dot(hid[...], full[i], preferred_element_type=F32)
        for k in range(2):
            p = proj[:, 128 * k : 128 * k + 128]
            at_k = pl.ds(pl.multiple_of(qi * 256 + 128 * k, 128), 128)
            out[:, at_k] = (wgt[...] * p).astype(BF16)
            term = cot[:, at_k].astype(F32) * p
            gp_acc[...] = term if not done and k == 0 else gp_acc[...] + term
        back = lax.dot_general(scaled[:, cols], full[i], (((1,), (1,)), ((), ())), preferred_element_type=F32)
        gh_acc[...] = back if not done else gh_acc[...] + back
        pltpu.make_async_copy(out.at[:, cols], out_h.at[:, cols], local.at[5]).start()
        done.append(i)

    far_first = (4, 3, -3, 2, -2, 1, -1)
    g_z, g_yz, g_yx, g_x, g_core = [group(1) for _ in range(5)]
    seven = pl.ds(0, 7)
    s_z, s_yz, s_yx = kind(recv_z.at[seven]), kind(recv_yz.at[seven]), kind(recv_yx.at[seven])
    s_x, s_core = kind(recv_x.at[pl.ds(0, 3)]), kind(core_r)
    none = jnp.zeros((8, 128), F32)

    def across_z():
        ends = ring_end(1)
        for k in range(8):
            send_z[k] = ends[k // 2][96 * (k % 2) : 96 * (k % 2) + 96].astype(BF16)
        for k in far_first:
            to = lax.rem(z + k + 8, 8)
            push(send_z.at[to], recv_z.at[z], s_z, g_z, at(dz=k))
        recv_z[z] = send_z[z]

    def across_y(send, recv, base, of):
        for k in far_first:
            to = lax.rem(yl + k + 4, 4)
            push(send.at[to], recv.at[y], of, base, at(dy=k))
        recv[y] = send[yl]

    def across_y_z():
        ends = ring_end(0)
        for k in range(4):
            rows = slice(24 * (k % 2), 24 * (k % 2) + 24)
            low_cols, high_cols = ends[k // 2][rows], ends[2 + k // 2][rows]
            parts = [low_cols[:, :128], low_cols[:, 128:], high_cols[:, :128], high_cols[:, 128:]]
            send_yz[k] = jnp.concatenate(parts, axis=0).astype(BF16)
        across_y(send_yz, recv_yz, g_yz, s_yz)

    def gathered(recv, base, n):
        arrive(recv.at[pl.ds(0, n - 1)], base)
        total = recv[0].astype(F32)
        for k in range(1, n):
            total = total + recv[k].astype(F32)
        return total

    def across_y_x():
        total = gathered(recv_z, g_z, 8)
        for k in range(4):
            send_yx[k] = jnp.concatenate([total[24 * k : 24 * k + 24], none], axis=0).astype(BF16)
        across_y(send_yx, recv_yx, g_yx, s_yx)

    def exchange_x():
        total_z = gathered(recv_yz, g_yz, 8)
        total_x = gathered(recv_yx, g_yx, 8)
        recv_x[x] = jnp.concatenate([total_z, total_x], axis=0).astype(BF16)
        for k in (2, 1, 3):
            push(recv_x.at[x], recv_x.at[x], s_x, g_x, at(dx=k))

    def exchange_core():
        total = gathered(recv_x, g_x, 4)
        core_s[pl.ds(0, 96), :] = total[:96]
        for k in range(4):
            core_s[pl.ds(96 + 24 * k, 24), :] = recv_x[k].astype(F32)[96:120]
        push(core_s, core_r, s_core, g_core, at(dc=1))

    def finish_sum():
        arrive(core_r, g_core)
        for h in range(2):
            f = jnp.where(first, core_s[...], core_r[...]) if h == 0 else jnp.where(first, core_r[...], core_s[...])
            for k in range(8):
                part = f[24 * k : 24 * k + 24]
                gw[:, pl.ds(h * (D // 2) + 128 * k, 128)] = jnp.where(first, part[:SHARD], part[SHARD:])
        copy = pltpu.make_async_copy(gw, gw_h, local.at[7])
        copy.start()
        stores.append(copy)

    cot_loads[1].wait()
    partials(c, own_z, own_x, (0, 1))
    ring_step(0, 1, True)
    partials(c, own_z, own_x, (2, 3))
    ring_step(1, 1, True)
    ring_step(0, 2, False)
    make_unit()
    ring_step(0, 2, True)
    ring_step(1, 2, False)
    ring_step(1, 2, True)
    ring_step(0, 3, False)
    ring_step(0, 3, True)
    along_y()
    spread(0)
    ring_step(0, 4, False)
    ring_step(0, 4, True)
    across_z()
    spread(1)
    spread(2)
    forward(0)
    across_y_z()
    spread(3)
    multiply(0)
    across_y_x()
    forward(1)
    forward(2)
    multiply(4)
    forward(3)
    multiply(1)
    multiply(3)
    exchange_x()
    last(0)
    last(1)
    last(2)
    last(3)
    multiply(5)
    multiply(7)
    exchange_core()
    multiply(2)
    multiply(6)
    finish_sum()
    gh[...] = gh_acc[...].astype(BF16)
    copy = pltpu.make_async_copy(gh, gh_h, local.at[6])
    copy.start()
    stores.append(copy)
    gp[...] = (live_row * jnp.sum(gp_acc[...].T, axis=0, keepdims=True)).reshape(ROWS)
    copy = pltpu.make_async_copy(gp, gp_h, local.at[8])
    copy.start()
    stores.append(copy)

    for copy in stores:
        copy.wait()
    pltpu.make_async_copy(out, out_h, local.at[5]).wait()
    assert len(sends) == KINDS and used[0] == SEMS
    for of, total in enumerate(sends):
        pltpu.make_async_remote_copy(
            total, total, ssem.at[of], rsem.at[0], device_id=at(dc=1), device_id_type=MESH
        ).wait_send()


def hand_over(*refs):
    n = (len(refs) - 1) // 2
    copies = [pltpu.make_async_copy(refs[i], refs[n + i], refs[-1].at[i]) for i in range(n)]
    for copy in copies:
        copy.start()
    for copy in copies:
        copy.wait()


def pin(a):
    return pltpu.with_memory_space_constraint(a, pltpu.HBM)


def body(hidden, prob, counts, down_weight, cotangent):
    hbm = pl.BlockSpec(memory_space=pltpu.HBM)
    free = pl.BlockSpec(memory_space=pl.ANY)
    vmem = pltpu.VMEM
    output, grad_hidden, grad_prob, grad_weight = pl.pallas_call(
        kernel,
        name="expert_down",
        out_shape=(
            jax.ShapeDtypeStruct((ROWS, D), BF16),
            jax.ShapeDtypeStruct((ROWS, FF), BF16),
            jax.ShapeDtypeStruct((ROWS,), F32),
            jax.ShapeDtypeStruct((SHARD, D), F32),
        ),
        in_specs=[hbm, hbm, pl.BlockSpec(memory_space=pltpu.SMEM), hbm, hbm],
        out_specs=(free, free, free, free),
        scratch_shapes=[
            vmem((ROWS, FF), BF16),
            vmem((FF, ROWS), BF16),
            vmem((ROWS, D), BF16),
            vmem((ROWS, D), BF16),
            vmem((ROWS,), F32),
            vmem((ROWS, 128), F32),
            vmem((8, 192, 256), BF16),
            vmem((4, FF, 128), BF16),
            vmem((8, 192, 256), BF16),
            vmem((4, FF, 128), BF16),
            vmem((8, 192, 256), BF16),
            vmem((4, FF, 128), BF16),
            vmem((28, 48, 256), BF16),
            vmem((12, 192, 128), BF16),
            vmem((SHARD, D), BF16),
            vmem((2, 16, D), BF16),
            vmem((2 * SHARD, 256), F32),
            vmem((8, 4, 8, 48, 128), BF16),
            vmem((8, FF, 256), BF16),
            vmem((ROWS, D), BF16),
            vmem((ROWS, FF), F32),
            vmem((ROWS, FF), BF16),
            vmem((ROWS, 128), F32),
            vmem((ROWS,), F32),
            vmem((8, 96, 128), BF16),
            vmem((8, 96, 128), BF16),
            vmem((4, 96, 128), BF16),
            vmem((8, 96, 128), BF16),
            vmem((4, 32, 128), BF16),
            vmem((8, 32, 128), BF16),
            vmem((4, 128, 128), BF16),
            vmem((192, 128), F32),
            vmem((192, 128), F32),
            vmem((SHARD, D), F32),
            pltpu.SemaphoreType.DMA((9,)),
            pltpu.SemaphoreType.DMA((KINDS,)),
            pltpu.SemaphoreType.DMA((SEMS,)),
        ],
        compiler_params=pltpu.CompilerParams(
            collective_id=0, has_side_effects=True, vmem_limit_bytes=40 * 2**20
        ),
    )(pin(hidden), pin(prob), counts, pin(down_weight), pin(cotangent))
    results = (output, grad_hidden, grad_prob, grad_weight)
    return pl.pallas_call(
        hand_over,
        name="hand_over",
        out_shape=tuple(jax.ShapeDtypeStruct(a.shape, a.dtype) for a in results),
        in_specs=[pl.BlockSpec(memory_space=pltpu.VMEM)] * 4,
        out_specs=(free,) * 4,
        scratch_shapes=[pltpu.SemaphoreType.DMA((4,))],
        compiler_params=pltpu.CompilerParams(vmem_limit_bytes=8 * 2**20),
    )(*results)


def solution(mesh):
    placed = (
        P(("rep", "shard"), None),
        P(("rep", "shard")),
        P(("rep", "shard")),
        P("shard", None),
        P(("rep", "shard"), None),
    )
    return jax.shard_map(
        body,
        mesh=mesh,
        in_specs=placed,
        out_specs=(
            P(("rep", "shard"), None),
            P(("rep", "shard"), None),
            P(("rep", "shard")),
            P("shard", None),
        ),
        check_vma=False,
    )
```

```python
import jax
import jax.numpy as jnp
from jax import lax
from jax.experimental import pallas as pl
from jax.experimental.pallas import tpu as pltpu
from jax.sharding import PartitionSpec as P

MESH = pl.DeviceIdType.MESH
F32, BF16 = jnp.float32, jnp.bfloat16
NX, NY, NZ, LO = 4, 8, 8, 4
ROWS, FF, D, SHARD = 384, 768, 2048, 12
SEMS, KINDS = 57, 14


def device(x, y, z, c):
    x, y, z, c = lax.rem(x, NX), lax.rem(y, NY), lax.rem(z, NZ), lax.rem(c, 2)
    return (lax.div(y, LO) * NX + x, z * (2 * LO) + lax.rem(y, LO) * 2 + c)


def kernel(
    hidden_h, prob_h, counts_s, weight_h, cot_h, out_h, gh_h, gp_h, gw_h,
    hid, hid_t, cot, scaled, prob, wgt, own_z, own_x, oth_z, oth_x, rcv_z, rcv_x, ring_z, ring_x, shard_in, z_mine, z_other, unit, order_z,
    blocks, full, out, gh_acc, gh, gp_acc, gp, send_z, recv_z, send_yz, recv_yz, send_yx, recv_yx, mix, send_x, recv_x, gw,
    local, ssem, rsem,
):
    r, s = lax.axis_index("rep"), lax.axis_index("shard")
    x, yh = lax.rem(r, NX), lax.div(r, NX)
    z, yl, c = lax.div(s, 2 * LO), lax.rem(lax.div(s, 2), LO), lax.rem(s, 2)
    y = yh * LO + yl
    first = c == 0

    def at(dx=0, dy=0, dz=0, dc=0):
        return device(x + dx + NX, y + dy + NY, z + dz + NZ, c + dc)

    loads = [
        pltpu.make_async_copy(a, b, local.at[i])
        for i, (a, b) in enumerate([(prob_h, prob), (hidden_h, hid), (weight_h, shard_in)])
    ]
    for load in loads:
        load.start()
    cot_loads = []
    for i, half in enumerate((1 - c, c)):
        cols = pl.ds(pl.multiple_of(half * (D // 2), D // 2), D // 2)
        load = pltpu.make_async_copy(cot_h.at[:, cols], cot.at[:, cols], local.at[3 + i])
        load.start()
        cot_loads.append(load)

    barrier = pltpu.get_barrier_semaphore()
    peers = [at(dc=1)] + [at(dx=k) for k in (1, 2, 3)]
    peers += [at(dx=k, dc=1) for k in (1, 2, 3)]
    peers += [at(dy=k) for k in range(1, 8)] + [at(dz=k) for k in range(1, 8)]
    for peer in peers:
        pl.semaphore_signal(barrier, inc=1, device_id=peer, device_id_type=MESH)

    used, sends = [0], []

    def group(n):
        used[0] += n
        assert used[0] <= SEMS
        return used[0] - n

    def kind(total):
        sends.append(total)
        return len(sends) - 1

    def push(src, dst, of, rsem_i, to):
        pltpu.make_async_remote_copy(
            src, dst, ssem.at[of], rsem.at[rsem_i], device_id=to, device_id_type=MESH
        ).start()

    def arrive(dst, rsem_i):
        pltpu.make_async_remote_copy(
            dst, dst, ssem.at[0], rsem.at[rsem_i], device_id=at(dc=1), device_id_type=MESH
        ).wait_recv()

    loads[0].wait()
    place = lax.broadcasted_iota(jnp.int32, (1, ROWS), 1)
    live_row = (place < counts_s[...].reshape(1, 1)).astype(F32)
    row = prob[...].reshape(1, ROWS) * live_row
    wgt[...] = jnp.broadcast_to(row, (128, ROWS)).T
    loads[1].wait()
    hid_t[...] = hid[...].T

    def partials(half, keep_z, keep_x, ns):
        for n in ns:
            start = half * (D // 2) + 256 * n
            cols = pl.ds(pl.multiple_of(start, 256), 256)
            two = jnp.concatenate([wgt[...], wgt[...]], axis=1)
            piece = (two * cot[:, cols].astype(F32)).astype(BF16)
            scaled[(4 if keep_z is own_z else 0) + n] = piece
            part = jnp.dot(hid_t[...], piece, preferred_element_type=F32)
            if n < 2:
                keep_z[:, pl.ds(96 * n, 96), :] = part.astype(BF16).reshape(8, 96, 256)
            else:
                for k in range(2):
                    keep_x[2 * (n - 2) + k] = part[:, 128 * k : 128 * k + 128].astype(BF16)

    orders = ([4, 3, -3, 2, -2, 1, -1, 0], [2, 1, -1, 0])
    place_of, length = (z, x), (NZ, NX)
    own, oth, rcv = (own_z, own_x), (oth_z, oth_x), (rcv_z, rcv_x)
    g_shard, g_pair = group(1), (group(8), group(4))
    s_shard, s_pair = kind(z_other), (kind(rcv_z), kind(rcv_x))

    def push_pair(a):
        for i, k in enumerate(orders[a]):
            dest = lax.rem(place_of[a] + k + length[a], length[a])
            push(oth[a].at[dest], rcv[a].at[dest], s_pair[a], g_pair[a] + i, at(dc=1))

    cot_loads[0].wait()
    partials(1 - c, oth_z, oth_x, (0, 1))
    loads[2].wait()
    for h in range(2):
        for b in range(2):
            cols = pl.ds(pl.multiple_of(h * (D // 2) + x * 256 + 128 * b, 128), 128)
            unit[pl.ds(24 * h + SHARD * b, SHARD), :] = shard_in[:, cols].astype(F32)
    z_mine[z] = unit[...].astype(BF16)
    qs = [c * 4 + lax.rem(x + k, 4) for k in range(4)] + [(1 - c) * 4 + lax.rem(x + k, 4) for k in range(4)]
    yls = [yl, lax.rem(yl + 3, 4), lax.rem(yl + 1, 4), lax.rem(yl + 2, 4)]
    low, high = pl.ds(0, 4), pl.ds(4, 4)
    g_wz, g_wy, g_wx, g_wf, g_wc = group(1), group(3), group(8), group(4), group(4)
    s_wz, s_wy, s_wx, s_wf, s_wc = [
        kind(t) for t in (z_mine.at[pl.ds(0, 7)], blocks.at[0, pl.ds(0, 3)], blocks.at[pl.ds(0, 2)], blocks.at[0], blocks.at[pl.ds(0, 4)])
    ]

    def send_unit():
        for k in (4, 3, -3, 2, -2, 1, -1):
            push(z_mine.at[z], z_mine.at[z], s_wz, g_wz, at(dz=k))

    def swap():
        arrive(z_mine.at[pl.ds(0, 7)], g_wz)
        push(z_mine, z_other, s_shard, g_shard, at(dc=1))

    def along_y():
        q = qs[0]
        arrive(z_other, g_shard)
        mine, others = z_mine[...].astype(F32), z_other[...].astype(F32)
        mine = jnp.where(first, mine[:, :24], mine[:, 24:])
        others = jnp.where(first, others[:, :24], others[:, 24:])
        even, odd = jnp.where(first, mine, others), jnp.where(first, others, mine)
        for b in range(2):
            from_b = slice(SHARD * b, SHARD * b + SHARD)
            order_z[:, pl.ds(24 * b, SHARD), :] = even[:, from_b]
            order_z[:, pl.ds(24 * b + SHARD, SHARD), :] = odd[:, from_b]
        blocks[q, yl] = order_z[...].astype(BF16)
        push(blocks.at[q, yl], blocks.at[q, yl], s_wy, g_wy, at(dy=1))
        push(blocks.at[q, yl], blocks.at[q, yl], s_wy, g_wy + 1, at(dy=-1))
        push(blocks.at[q, yl, low], blocks.at[q, yl, low], s_wy, g_wy + 2, at(dy=2))
        push(blocks.at[q, yl, high], blocks.at[q, yl, high], s_wy, g_wy + 2, at(dy=-2))

    pl.semaphore_wait(barrier, len(peers))
    send_unit()
    push_pair(0)
    partials(1 - c, oth_z, oth_x, (2, 3))
    push_pair(1)

    paired = set()

    def pair(a, k):
        k = length[a] // 2 if k == -length[a] // 2 else k
        dest = lax.rem(place_of[a] + k + length[a], length[a])
        if (a, k) not in paired:
            paired.add((a, k))
            arrive(rcv[a].at[dest], g_pair[a] + orders[a].index(k))
        return dest

    rings, height = (ring_z, ring_x), (96, 384)
    g_ring = (group(14), group(6))
    s_ring = (kind(ring_z), kind(ring_x))

    def slot(a, d, i, t, far):
        return d if t == 1 else 2 + 4 * (t - 2) + 2 * far + d

    def ring_step(a, t, far):
        for i in range(1):
            for d in range(2):
                sub = d if far else 1 - d
                dest = pair(a, (length[a] // 2 + 1 - t) * (1 if d == 0 else -1))
                rows = pl.ds(height[a] * sub, height[a])
                total = own[a][dest, rows, :].astype(F32) + rcv[a][dest, rows, :].astype(F32)
                if t > 2 or (t == 2 and far):
                    m = slot(a, d, i, t - 1, far)
                    arrive(rings[a].at[m], g_ring[a] + m)
                    total = total + rings[a][m].astype(F32)
                own[a][dest, rows, :] = total.astype(BF16)
                m = slot(a, d, i, t, far)
                step = 1 if d == 0 else -1
                push(own[a].at[dest, rows, :], rings[a].at[m], s_ring[a], g_ring[a] + m,
                     at(dz=step) if a == 0 else at(dx=step))

    def ring_end(a):
        dest = pair(a, 0)
        ends = []
        for sub in range(2):
            rows = pl.ds(height[a] * sub, height[a])
            ends.append(own[a][dest, rows, :].astype(F32) + rcv[a][dest, rows, :].astype(F32))
        for far in (False, True):
            for i in range(1):
                for d in range(2):
                    sub = d if far else 1 - d
                    m = slot(a, d, i, length[a] // 2, far)
                    arrive(rings[a].at[m], g_ring[a] + m)
                    ends[sub] = ends[sub] + rings[a][m].astype(F32)
        return ends

    def to_core(k, j):
        block = blocks.at[qs[k], yls[j]]
        push(block, block, s_wc, g_wc + k, at(dc=1))

    def spread(j):
        if j in (1, 2):
            arrive(blocks.at[qs[0], yls[j]], g_wy + j - 1)
        if j == 3:
            arrive(blocks.at[qs[0], yls[3]], g_wy + 2)
        block = blocks.at[qs[0], yls[j]]
        push(block, block, s_wx, g_wx + j, at(dx=1))
        push(block, block, s_wx, g_wx + 4 + j, at(dx=-1))
        to_core(0, j)

    def forward(j):
        arrive(blocks.at[qs[3], yls[j]], g_wx + j)
        part = blocks.at[qs[3], yls[j], low]
        push(part, part, s_wf, g_wf + j, at(dx=1))
        arrive(blocks.at[qs[1], yls[j]], g_wx + 4 + j)
        part = blocks.at[qs[1], yls[j], high]
        push(part, part, s_wf, g_wf + j, at(dx=-1))
        to_core(3, j)
        to_core(1, j)

    def last(j):
        arrive(blocks.at[qs[2], yls[j]], g_wf + j)
        to_core(2, j)

    stores, done = [], []

    def multiply(i):
        if i >= 4:
            arrive(blocks.at[qs[i]], g_wc + i - 4)
        qi = qs[i]
        for zi in range(8):
            for h in range(2):
                rows = [blocks[qi, k, zi].astype(F32)[24 * h : 24 * h + 24] for k in range(4)]
                full[i, pl.ds(96 * zi, 96), pl.ds(128 * h, 128)] = jnp.concatenate(rows, axis=0).astype(BF16)
        cols = pl.ds(pl.multiple_of(qi * 256, 256), 256)
        proj = jnp.dot(hid[...], full[i], preferred_element_type=F32)
        for k in range(2):
            p = proj[:, 128 * k : 128 * k + 128]
            at_k = pl.ds(pl.multiple_of(qi * 256 + 128 * k, 128), 128)
            out[:, at_k] = (wgt[...] * p).astype(BF16)
            term = cot[:, at_k].astype(F32) * p
            gp_acc[...] = term if not done and k == 0 else gp_acc[...] + term
        back = lax.dot_general(scaled[(4 if i < 4 else 0) + lax.rem(qi, 4)], full[i], (((1,), (1,)), ((), ())), preferred_element_type=F32)
        gh_acc[...] = back if not done else gh_acc[...] + back
        pltpu.make_async_copy(out.at[:, cols], out_h.at[:, cols], local.at[5]).start()
        done.append(i)

    far_first = (4, 3, -3, 2, -2, 1, -1)
    g_z, g_yz, g_yx, g_x = [group(1) for _ in range(4)]
    seven = pl.ds(0, 7)
    s_z, s_yz, s_yx = kind(recv_z.at[seven]), kind(recv_yz.at[seven]), kind(recv_yx.at[seven])
    s_x = kind(recv_x.at[seven])
    none = jnp.zeros((8, 128), F32)

    def across_z():
        ends = ring_end(1)
        for k in range(8):
            send_z[k] = ends[k // 4][96 * (k % 4) : 96 * (k % 4) + 96].astype(BF16)
        for k in far_first:
            to = lax.rem(z + k + 8, 8)
            push(send_z.at[to], recv_z.at[z], s_z, g_z, at(dz=k))
        recv_z[z] = send_z[z]

    def across_y(send, recv, base, of):
        for k in far_first:
            to = lax.rem(yl + k + 4, 4)
            push(send.at[to], recv.at[y], of, base, at(dy=k))
        recv[y] = send[yl]

    def across_y_z():
        ends = ring_end(0)
        for k in range(4):
            rows = slice(24 * k, 24 * k + 24)
            low_cols, high_cols = ends[0][rows], ends[1][rows]
            parts = [low_cols[:, :128], low_cols[:, 128:], high_cols[:, :128], high_cols[:, 128:]]
            send_yz[k] = jnp.concatenate(parts, axis=0).astype(BF16)
        across_y(send_yz, recv_yz, g_yz, s_yz)

    def gathered(recv, base, n):
        arrive(recv.at[pl.ds(0, n - 1)], base)
        total = recv[0].astype(F32)
        for k in range(1, n):
            total = total + recv[k].astype(F32)
        return total

    def across_y_x():
        total = gathered(recv_z, g_z, 8)
        for k in range(4):
            send_yx[k] = jnp.concatenate([total[24 * k : 24 * k + 24], none], axis=0).astype(BF16)
        across_y(send_yx, recv_yx, g_yx, s_yx)

    def exchange_x():
        total_z = gathered(recv_yz, g_yz, 8)
        total_x = gathered(recv_yx, g_yx, 8)
        for d in range(2):
            for k in range(4):
                mix[d, pl.ds(SHARD * k, SHARD), :] = total_z[24 * k + SHARD * d : 24 * k + SHARD * d + SHARD]
            mix[d, pl.ds(4 * SHARD, SHARD), :] = total_x[SHARD * d : SHARD * d + SHARD]
            mix[d, pl.ds(5 * SHARD, 4), :] = jnp.zeros((4, 128), F32)
        send_x[...] = mix[...].astype(BF16)
        here = recv_x.at[c * 4 + x]
        for k in (2, 1, 3):
            push(send_x.at[1 - c], here, s_x, g_x, at(dx=k, dc=1))
        for k in (2, 1, 3):
            push(send_x.at[c], here, s_x, g_x, at(dx=k))
        push(send_x.at[1 - c], here, s_x, g_x, at(dc=1))
        recv_x[c * 4 + x] = send_x[c]

    def finish_sum():
        arrive(recv_x.at[seven], g_x)
        for h in range(2):
            parts = [recv_x[4 * h + k].astype(F32) for k in range(4)]
            total = parts[0] + parts[1] + parts[2] + parts[3]
            for k in range(4):
                gw[:, pl.ds(h * (D // 2) + 128 * k, 128)] = total[SHARD * k : SHARD * k + SHARD]
                gw[:, pl.ds(h * (D // 2) + 512 + 128 * k, 128)] = parts[k][4 * SHARD : 5 * SHARD]
        copy = pltpu.make_async_copy(gw, gw_h, local.at[7])
        copy.start()
        stores.append(copy)

    def finish_rest():
        gh[...] = gh_acc[...].astype(BF16)
        copy = pltpu.make_async_copy(gh, gh_h, local.at[6])
        copy.start()
        stores.append(copy)
        gp[...] = (live_row * jnp.sum(gp_acc[...].T, axis=0, keepdims=True)).reshape(ROWS)
        copy = pltpu.make_async_copy(gp, gp_h, local.at[8])
        copy.start()
        stores.append(copy)

    cot_loads[1].wait()
    partials(c, own_z, own_x, (0, 1))
    ring_step(0, 1, True)
    partials(c, own_z, own_x, (2, 3))
    ring_step(1, 1, True)
    ring_step(0, 2, False)
    ring_step(0, 2, True)
    ring_step(1, 2, False)
    ring_step(1, 2, True)
    swap()
    ring_step(0, 3, False)
    ring_step(0, 3, True)
    along_y()
    spread(0)
    ring_step(0, 4, False)
    ring_step(0, 4, True)
    across_z()
    spread(1)
    spread(2)
    forward(0)
    spread(3)
    across_y_z()
    multiply(0)
    forward(1)
    across_y_x()
    forward(2)
    multiply(4)
    forward(3)
    multiply(1)
    exchange_x()
    multiply(3)
    last(0)
    last(1)
    last(2)
    multiply(5)
    last(3)
    multiply(7)
    multiply(2)
    multiply(6)
    finish_rest()
    finish_sum()
    for copy in stores:
        copy.wait()
    pltpu.make_async_copy(out, out_h, local.at[5]).wait()
    assert len(sends) == KINDS and used[0] == SEMS
    for of, total in enumerate(sends):
        pltpu.make_async_remote_copy(
            total, total, ssem.at[of], rsem.at[0], device_id=at(dc=1), device_id_type=MESH
        ).wait_send()


def hand_over(*refs):
    n = (len(refs) - 1) // 2
    copies = [pltpu.make_async_copy(refs[i], refs[n + i], refs[-1].at[i]) for i in range(n)]
    for copy in copies:
        copy.start()
    for copy in copies:
        copy.wait()


def pin(a):
    return pltpu.with_memory_space_constraint(a, pltpu.HBM)


def body(hidden, prob, counts, down_weight, cotangent):
    hbm = pl.BlockSpec(memory_space=pltpu.HBM)
    free = pl.BlockSpec(memory_space=pl.ANY)
    vmem = pltpu.VMEM
    output, grad_hidden, grad_prob, grad_weight = pl.pallas_call(
        kernel,
        name="expert_down",
        out_shape=(
            jax.ShapeDtypeStruct((ROWS, D), BF16),
            jax.ShapeDtypeStruct((ROWS, FF), BF16),
            jax.ShapeDtypeStruct((ROWS,), F32),
            jax.ShapeDtypeStruct((SHARD, D), F32),
        ),
        in_specs=[hbm, hbm, pl.BlockSpec(memory_space=pltpu.VMEM), hbm, hbm],
        out_specs=(free, free, free, free),
        scratch_shapes=[
            vmem((ROWS, FF), BF16),
            vmem((FF, ROWS), BF16),
            vmem((ROWS, D), BF16),
            vmem((8, ROWS, 256), BF16),
            vmem((ROWS,), F32),
            vmem((ROWS, 128), F32),
            vmem((8, 192, 256), BF16),
            vmem((4, FF, 128), BF16),
            vmem((8, 192, 256), BF16),
            vmem((4, FF, 128), BF16),
            vmem((8, 192, 256), BF16),
            vmem((4, FF, 128), BF16),
            vmem((14, 96, 256), BF16),
            vmem((6, 384, 128), BF16),
            vmem((SHARD, D), BF16),
            vmem((8, 48, 128), BF16),
            vmem((8, 48, 128), BF16),
            vmem((48, 128), F32),
            vmem((8, 48, 128), F32),
            vmem((8, 4, 8, 48, 128), BF16),
            vmem((8, FF, 256), BF16),
            vmem((ROWS, D), BF16),
            vmem((ROWS, FF), F32),
            vmem((ROWS, FF), BF16),
            vmem((ROWS, 128), F32),
            vmem((ROWS,), F32),
            vmem((8, 96, 128), BF16),
            vmem((8, 96, 128), BF16),
            vmem((4, 96, 128), BF16),
            vmem((8, 96, 128), BF16),
            vmem((4, 32, 128), BF16),
            vmem((8, 32, 128), BF16),
            vmem((2, 64, 128), F32),
            vmem((2, 64, 128), BF16),
            vmem((8, 64, 128), BF16),
            vmem((SHARD, D), F32),
            pltpu.SemaphoreType.DMA((9,)),
            pltpu.SemaphoreType.DMA((KINDS,)),
            pltpu.SemaphoreType.DMA((SEMS,)),
        ],
        compiler_params=pltpu.CompilerParams(
            collective_id=0, has_side_effects=True, vmem_limit_bytes=40 * 2**20
        ),
    )(pin(hidden), pin(prob), counts, pin(down_weight), pin(cotangent))
    results = (output, grad_hidden, grad_prob, grad_weight)
    return pl.pallas_call(
        hand_over,
        name="hand_over",
        out_shape=tuple(jax.ShapeDtypeStruct(a.shape, a.dtype) for a in results),
        in_specs=[pl.BlockSpec(memory_space=pltpu.VMEM)] * 4,
        out_specs=(free,) * 4,
        scratch_shapes=[pltpu.SemaphoreType.DMA((4,))],
        compiler_params=pltpu.CompilerParams(vmem_limit_bytes=8 * 2**20),
    )(*results)


def solution(mesh):
    placed = (
        P(("rep", "shard"), None),
        P(("rep", "shard")),
        P(("rep", "shard")),
        P("shard", None),
        P(("rep", "shard"), None),
    )
    return jax.shard_map(
        body,
        mesh=mesh,
        in_specs=placed,
        out_specs=(
            P(("rep", "shard"), None),
            P(("rep", "shard"), None),
            P(("rep", "shard")),
            P("shard", None),
        ),
        check_vma=False,
    )
```

```python
import jax
import jax.numpy as jnp
from jax import lax
from jax.experimental import pallas as pl
from jax.experimental.pallas import tpu as pltpu
from jax.sharding import PartitionSpec as P

MESH = pl.DeviceIdType.MESH
F32, BF16 = jnp.float32, jnp.bfloat16
NX, NY, NZ, LO = 4, 8, 8, 4
ROWS, FF, D, SHARD = 384, 768, 2048, 12
SEMS, KINDS = 57, 14


def device(x, y, z, c):
    x, y, z, c = lax.rem(x, NX), lax.rem(y, NY), lax.rem(z, NZ), lax.rem(c, 2)
    return (lax.div(y, LO) * NX + x, z * (2 * LO) + lax.rem(y, LO) * 2 + c)


def kernel(
    hidden_h, prob_h, counts_s, weight_h, cot_h, out_h, gh_h, gp_h, gw_h,
    hid, hid_t, cot, scaled, prob, wgt, own_z, own_x, oth_z, oth_x, rcv_z, rcv_x, ring_z, ring_x, shard_in, z_mine, z_other, unit, order_z,
    blocks, full, out, gh_acc, gh, gp_acc, gp, send_z, recv_z, send_yz, recv_yz, send_yx, recv_yx, mix, send_x, recv_x, gw,
    local, ssem, rsem,
):
    r, s = lax.axis_index("rep"), lax.axis_index("shard")
    x, yh = lax.rem(r, NX), lax.div(r, NX)
    z, yl, c = lax.div(s, 2 * LO), lax.rem(lax.div(s, 2), LO), lax.rem(s, 2)
    y = yh * LO + yl
    first = c == 0

    def at(dx=0, dy=0, dz=0, dc=0):
        return device(x + dx + NX, y + dy + NY, z + dz + NZ, c + dc)

    loads = [
        pltpu.make_async_copy(a, b, local.at[i])
        for i, (a, b) in enumerate([(prob_h, prob), (hidden_h, hid), (weight_h, shard_in)])
    ]
    for load in loads:
        load.start()
    cot_loads = []
    for i, half in enumerate((1 - c, c)):
        cols = pl.ds(pl.multiple_of(half * (D // 2), D // 2), D // 2)
        load = pltpu.make_async_copy(cot_h.at[:, cols], cot.at[:, cols], local.at[3 + i])
        load.start()
        cot_loads.append(load)

    barrier = pltpu.get_barrier_semaphore()
    peers = [at(dc=1)] + [at(dx=k) for k in (1, 2, 3)]
    peers += [at(dx=k, dc=1) for k in (1, 2, 3)]
    peers += [at(dy=k) for k in range(1, 8)] + [at(dz=k) for k in range(1, 8)]
    for peer in peers:
        pl.semaphore_signal(barrier, inc=1, device_id=peer, device_id_type=MESH)

    used, sends = [0], []

    def group(n):
        used[0] += n
        assert used[0] <= SEMS
        return used[0] - n

    def kind(total):
        sends.append(total)
        return len(sends) - 1

    def push(src, dst, of, rsem_i, to):
        pltpu.make_async_remote_copy(
            src, dst, ssem.at[of], rsem.at[rsem_i], device_id=to, device_id_type=MESH
        ).start()

    def arrive(dst, rsem_i):
        pltpu.make_async_remote_copy(
            dst, dst, ssem.at[0], rsem.at[rsem_i], device_id=at(dc=1), device_id_type=MESH
        ).wait_recv()

    loads[0].wait()
    place = lax.broadcasted_iota(jnp.int32, (1, ROWS), 1)
    live_row = (place < counts_s[...].reshape(1, 1)).astype(F32)
    row = prob[...].reshape(1, ROWS) * live_row
    wgt[...] = jnp.broadcast_to(row, (128, ROWS)).T
    loads[1].wait()
    hid_t[...] = hid[...].T

    def partials(half, keep_z, keep_x, ns):
        for n in ns:
            start = half * (D // 2) + 256 * n
            cols = pl.ds(pl.multiple_of(start, 256), 256)
            two = jnp.concatenate([wgt[...], wgt[...]], axis=1)
            piece = (two * cot[:, cols].astype(F32)).astype(BF16)
            scaled[(4 if keep_z is own_z else 0) + n] = piece
            part = jnp.dot(hid_t[...], piece, preferred_element_type=F32)
            if n < 2:
                keep_z[:, pl.ds(96 * n, 96), :] = part.astype(BF16).reshape(8, 96, 256)
            else:
                for k in range(2):
                    keep_x[2 * (n - 2) + k] = part[:, 128 * k : 128 * k + 128].astype(BF16)

    orders = ([4, 3, -3, 2, -2, 1, -1, 0], [2, 1, -1, 0])
    place_of, length = (z, x), (NZ, NX)
    own, oth, rcv = (own_z, own_x), (oth_z, oth_x), (rcv_z, rcv_x)
    g_shard, g_pair = group(1), (group(8), group(4))
    s_shard, s_pair = kind(z_other), (kind(rcv_z), kind(rcv_x))

    def push_pair(a):
        for i, k in enumerate(orders[a]):
            dest = lax.rem(place_of[a] + k + length[a], length[a])
            push(oth[a].at[dest], rcv[a].at[dest], s_pair[a], g_pair[a] + i, at(dc=1))

    cot_loads[0].wait()
    partials(1 - c, oth_z, oth_x, (0, 1))
    loads[2].wait()
    for h in range(2):
        for b in range(2):
            cols = pl.ds(pl.multiple_of(h * (D // 2) + x * 256 + 128 * b, 128), 128)
            unit[pl.ds(24 * h + SHARD * b, SHARD), :] = shard_in[:, cols].astype(F32)
    z_mine[z] = unit[...].astype(BF16)
    qs = [c * 4 + lax.rem(x + k, 4) for k in range(4)] + [(1 - c) * 4 + lax.rem(x + k, 4) for k in range(4)]
    yls = [yl, lax.rem(yl + 3, 4), lax.rem(yl + 1, 4), lax.rem(yl + 2, 4)]
    low, high = pl.ds(0, 4), pl.ds(4, 4)
    g_wz, g_wy, g_wx, g_wf, g_wc = group(1), group(3), group(8), group(4), group(4)
    s_wz, s_wy, s_wx, s_wf, s_wc = [
        kind(t) for t in (z_mine.at[pl.ds(0, 7)], blocks.at[0, pl.ds(0, 3)], blocks.at[pl.ds(0, 2)], blocks.at[0], blocks.at[pl.ds(0, 4)])
    ]

    def send_unit():
        for k in (4, 3, -3, 2, -2, 1, -1):
            push(z_mine.at[z], z_mine.at[z], s_wz, g_wz, at(dz=k))

    def swap():
        arrive(z_mine.at[pl.ds(0, 7)], g_wz)
        push(z_mine, z_other, s_shard, g_shard, at(dc=1))

    def along_y():
        q = qs[0]
        arrive(z_other, g_shard)
        mine, others = z_mine[...].astype(F32), z_other[...].astype(F32)
        mine = jnp.where(first, mine[:, :24], mine[:, 24:])
        others = jnp.where(first, others[:, :24], others[:, 24:])
        even, odd = jnp.where(first, mine, others), jnp.where(first, others, mine)
        for b in range(2):
            from_b = slice(SHARD * b, SHARD * b + SHARD)
            order_z[:, pl.ds(24 * b, SHARD), :] = even[:, from_b]
            order_z[:, pl.ds(24 * b + SHARD, SHARD), :] = odd[:, from_b]
        blocks[q, yl] = order_z[...].astype(BF16)
        push(blocks.at[q, yl], blocks.at[q, yl], s_wy, g_wy, at(dy=1))
        push(blocks.at[q, yl], blocks.at[q, yl], s_wy, g_wy + 1, at(dy=-1))
        push(blocks.at[q, yl, low], blocks.at[q, yl, low], s_wy, g_wy + 2, at(dy=2))
        push(blocks.at[q, yl, high], blocks.at[q, yl, high], s_wy, g_wy + 2, at(dy=-2))

    pl.semaphore_wait(barrier, len(peers))
    send_unit()
    push_pair(0)
    partials(1 - c, oth_z, oth_x, (2, 3))
    push_pair(1)

    paired = set()

    def pair(a, k):
        k = length[a] // 2 if k == -length[a] // 2 else k
        dest = lax.rem(place_of[a] + k + length[a], length[a])
        if (a, k) not in paired:
            paired.add((a, k))
            arrive(rcv[a].at[dest], g_pair[a] + orders[a].index(k))
        return dest

    rings, height = (ring_z, ring_x), (96, 384)
    g_ring = (group(14), group(6))
    s_ring = (kind(ring_z), kind(ring_x))

    def slot(a, d, i, t, far):
        return d if t == 1 else 2 + 4 * (t - 2) + 2 * far + d

    def ring_step(a, t, far):
        for i in range(1):
            for d in range(2):
                sub = d if far else 1 - d
                dest = pair(a, (length[a] // 2 + 1 - t) * (1 if d == 0 else -1))
                rows = pl.ds(height[a] * sub, height[a])
                total = own[a][dest, rows, :].astype(F32) + rcv[a][dest, rows, :].astype(F32)
                if t > 2 or (t == 2 and far):
                    m = slot(a, d, i, t - 1, far)
                    arrive(rings[a].at[m], g_ring[a] + m)
                    total = total + rings[a][m].astype(F32)
                own[a][dest, rows, :] = total.astype(BF16)
                m = slot(a, d, i, t, far)
                step = 1 if d == 0 else -1
                push(own[a].at[dest, rows, :], rings[a].at[m], s_ring[a], g_ring[a] + m,
                     at(dz=step) if a == 0 else at(dx=step))

    def ring_end(a):
        dest = pair(a, 0)
        ends = []
        for sub in range(2):
            rows = pl.ds(height[a] * sub, height[a])
            ends.append(own[a][dest, rows, :].astype(F32) + rcv[a][dest, rows, :].astype(F32))
        for far in (False, True):
            for i in range(1):
                for d in range(2):
                    sub = d if far else 1 - d
                    m = slot(a, d, i, length[a] // 2, far)
                    arrive(rings[a].at[m], g_ring[a] + m)
                    ends[sub] = ends[sub] + rings[a][m].astype(F32)
        return ends

    def to_core(k, j):
        block = blocks.at[qs[k], yls[j]]
        push(block, block, s_wc, g_wc + k, at(dc=1))

    def spread(j):
        if j in (1, 2):
            arrive(blocks.at[qs[0], yls[j]], g_wy + j - 1)
        if j == 3:
            arrive(blocks.at[qs[0], yls[3]], g_wy + 2)
        block = blocks.at[qs[0], yls[j]]
        push(block, block, s_wx, g_wx + j, at(dx=1))
        push(block, block, s_wx, g_wx + 4 + j, at(dx=-1))
        to_core(0, j)

    def forward(j):
        arrive(blocks.at[qs[3], yls[j]], g_wx + j)
        part = blocks.at[qs[3], yls[j], low]
        push(part, part, s_wf, g_wf + j, at(dx=1))
        arrive(blocks.at[qs[1], yls[j]], g_wx + 4 + j)
        part = blocks.at[qs[1], yls[j], high]
        push(part, part, s_wf, g_wf + j, at(dx=-1))
        to_core(3, j)
        to_core(1, j)

    def last(j):
        arrive(blocks.at[qs[2], yls[j]], g_wf + j)
        to_core(2, j)

    stores, done = [], []

    def multiply(i):
        if i >= 4:
            arrive(blocks.at[qs[i]], g_wc + i - 4)
        qi = qs[i]
        for zi in range(8):
            for h in range(2):
                rows = [blocks[qi, k, zi].astype(F32)[24 * h : 24 * h + 24] for k in range(4)]
                full[i, pl.ds(96 * zi, 96), pl.ds(128 * h, 128)] = jnp.concatenate(rows, axis=0).astype(BF16)
        cols = pl.ds(pl.multiple_of(qi * 256, 256), 256)
        proj = jnp.dot(hid[...], full[i], preferred_element_type=F32)
        for k in range(2):
            p = proj[:, 128 * k : 128 * k + 128]
            at_k = pl.ds(pl.multiple_of(qi * 256 + 128 * k, 128), 128)
            out[:, at_k] = (wgt[...] * p).astype(BF16)
            term = cot[:, at_k].astype(F32) * p
            gp_acc[...] = term if not done and k == 0 else gp_acc[...] + term
        back = lax.dot_general(scaled[(4 if i < 4 else 0) + lax.rem(qi, 4)], full[i], (((1,), (1,)), ((), ())), preferred_element_type=F32)
        if len(done) == 7:
            gh[...] = (gh_acc[...] + back).astype(BF16)
        else:
            gh_acc[...] = back if not done else gh_acc[...] + back
        pltpu.make_async_copy(out.at[:, cols], out_h.at[:, cols], local.at[5]).start()
        done.append(i)

    far_first = (4, 3, -3, 2, -2, 1, -1)
    g_z, g_yz, g_yx, g_x = [group(1) for _ in range(4)]
    seven = pl.ds(0, 7)
    s_z, s_yz, s_yx = kind(recv_z.at[seven]), kind(recv_yz.at[seven]), kind(recv_yx.at[seven])
    s_x = kind(recv_x.at[seven])
    none = jnp.zeros((8, 128), F32)

    def across_z():
        ends = ring_end(1)
        for k in range(8):
            send_z[k] = ends[k // 4][96 * (k % 4) : 96 * (k % 4) + 96].astype(BF16)
        for k in far_first:
            to = lax.rem(z + k + 8, 8)
            push(send_z.at[to], recv_z.at[z], s_z, g_z, at(dz=k))
        recv_z[z] = send_z[z]

    def across_y(send, recv, base, of):
        for k in far_first:
            to = lax.rem(yl + k + 4, 4)
            push(send.at[to], recv.at[y], of, base, at(dy=k))
        recv[y] = send[yl]

    def across_y_z():
        ends = ring_end(0)
        for k in range(4):
            rows = slice(24 * k, 24 * k + 24)
            low_cols, high_cols = ends[0][rows], ends[1][rows]
            parts = [low_cols[:, :128], low_cols[:, 128:], high_cols[:, :128], high_cols[:, 128:]]
            send_yz[k] = jnp.concatenate(parts, axis=0).astype(BF16)
        across_y(send_yz, recv_yz, g_yz, s_yz)

    def gathered(recv, base, n):
        arrive(recv.at[pl.ds(0, n - 1)], base)
        total = recv[0].astype(F32)
        for k in range(1, n):
            total = total + recv[k].astype(F32)
        return total

    def across_y_x():
        total = gathered(recv_z, g_z, 8)
        for k in range(4):
            send_yx[k] = jnp.concatenate([total[24 * k : 24 * k + 24], none], axis=0).astype(BF16)
        across_y(send_yx, recv_yx, g_yx, s_yx)

    def exchange_x():
        total_z = gathered(recv_yz, g_yz, 8)
        total_x = gathered(recv_yx, g_yx, 8)
        for d in range(2):
            for k in range(4):
                mix[d, pl.ds(SHARD * k, SHARD), :] = total_z[24 * k + SHARD * d : 24 * k + SHARD * d + SHARD]
            mix[d, pl.ds(4 * SHARD, SHARD), :] = total_x[SHARD * d : SHARD * d + SHARD]
            mix[d, pl.ds(5 * SHARD, 4), :] = jnp.zeros((4, 128), F32)
        send_x[...] = mix[...].astype(BF16)
        here = recv_x.at[c * 4 + x]
        for k in (2, 1, 3):
            push(send_x.at[1 - c], here, s_x, g_x, at(dx=k, dc=1))
        for k in (2, 1, 3):
            push(send_x.at[c], here, s_x, g_x, at(dx=k))
        push(send_x.at[1 - c], here, s_x, g_x, at(dc=1))
        recv_x[c * 4 + x] = send_x[c]

    def finish_sum():
        arrive(recv_x.at[seven], g_x)
        for h in range(2):
            parts = [recv_x[4 * h + k].astype(F32) for k in range(4)]
            total = parts[0] + parts[1] + parts[2] + parts[3]
            for k in range(4):
                gw[:, pl.ds(h * (D // 2) + 128 * k, 128)] = total[SHARD * k : SHARD * k + SHARD]
                gw[:, pl.ds(h * (D // 2) + 512 + 128 * k, 128)] = parts[k][4 * SHARD : 5 * SHARD]
        copy = pltpu.make_async_copy(gw, gw_h, local.at[7])
        copy.start()
        stores.append(copy)

    def finish_rest():
        copy = pltpu.make_async_copy(gh, gh_h, local.at[6])
        copy.start()
        stores.append(copy)
        gp[...] = (live_row * jnp.sum(gp_acc[...].T, axis=0, keepdims=True)).reshape(ROWS)
        copy = pltpu.make_async_copy(gp, gp_h, local.at[8])
        copy.start()
        stores.append(copy)

    cot_loads[1].wait()
    partials(c, own_z, own_x, (0, 1))
    ring_step(0, 1, True)
    partials(c, own_z, own_x, (2, 3))
    ring_step(1, 1, True)
    ring_step(0, 2, False)
    ring_step(0, 2, True)
    ring_step(1, 2, False)
    ring_step(1, 2, True)
    swap()
    ring_step(0, 3, False)
    ring_step(0, 3, True)
    along_y()
    spread(0)
    ring_step(0, 4, False)
    ring_step(0, 4, True)
    across_z()
    spread(1)
    spread(2)
    forward(0)
    spread(3)
    across_y_z()
    multiply(0)
    forward(1)
    forward(2)
    across_y_x()
    multiply(4)
    forward(3)
    multiply(1)
    exchange_x()
    multiply(3)
    last(0)
    last(1)
    last(2)
    multiply(5)
    last(3)
    multiply(7)
    multiply(2)
    multiply(6)
    finish_rest()
    finish_sum()
    for copy in stores:
        copy.wait()
    pltpu.make_async_copy(out, out_h, local.at[5]).wait()
    assert len(sends) == KINDS and used[0] == SEMS
    for of, total in enumerate(sends):
        pltpu.make_async_remote_copy(
            total, total, ssem.at[of], rsem.at[0], device_id=at(dc=1), device_id_type=MESH
        ).wait_send()


def hand_over(*refs):
    n = (len(refs) - 1) // 2
    copies = [pltpu.make_async_copy(refs[i], refs[n + i], refs[-1].at[i]) for i in range(n)]
    for copy in copies:
        copy.start()
    for copy in copies:
        copy.wait()


def pin(a):
    return pltpu.with_memory_space_constraint(a, pltpu.HBM)


def body(hidden, prob, counts, down_weight, cotangent):
    hbm = pl.BlockSpec(memory_space=pltpu.HBM)
    free = pl.BlockSpec(memory_space=pl.ANY)
    vmem = pltpu.VMEM
    output, grad_hidden, grad_prob, grad_weight = pl.pallas_call(
        kernel,
        name="expert_down",
        out_shape=(
            jax.ShapeDtypeStruct((ROWS, D), BF16),
            jax.ShapeDtypeStruct((ROWS, FF), BF16),
            jax.ShapeDtypeStruct((ROWS,), F32),
            jax.ShapeDtypeStruct((SHARD, D), F32),
        ),
        in_specs=[hbm, hbm, pl.BlockSpec(memory_space=pltpu.VMEM), hbm, hbm],
        out_specs=(free, free, free, free),
        scratch_shapes=[
            vmem((ROWS, FF), BF16),
            vmem((FF, ROWS), BF16),
            vmem((ROWS, D), BF16),
            vmem((8, ROWS, 256), BF16),
            vmem((ROWS,), F32),
            vmem((ROWS, 128), F32),
            vmem((8, 192, 256), BF16),
            vmem((4, FF, 128), BF16),
            vmem((8, 192, 256), BF16),
            vmem((4, FF, 128), BF16),
            vmem((8, 192, 256), BF16),
            vmem((4, FF, 128), BF16),
            vmem((14, 96, 256), BF16),
            vmem((6, 384, 128), BF16),
            vmem((SHARD, D), BF16),
            vmem((8, 48, 128), BF16),
            vmem((8, 48, 128), BF16),
            vmem((48, 128), F32),
            vmem((8, 48, 128), F32),
            vmem((8, 4, 8, 48, 128), BF16),
            vmem((8, FF, 256), BF16),
            vmem((ROWS, D), BF16),
            vmem((ROWS, FF), F32),
            vmem((ROWS, FF), BF16),
            vmem((ROWS, 128), F32),
            vmem((ROWS,), F32),
            vmem((8, 96, 128), BF16),
            vmem((8, 96, 128), BF16),
            vmem((4, 96, 128), BF16),
            vmem((8, 96, 128), BF16),
            vmem((4, 32, 128), BF16),
            vmem((8, 32, 128), BF16),
            vmem((2, 64, 128), F32),
            vmem((2, 64, 128), BF16),
            vmem((8, 64, 128), BF16),
            vmem((SHARD, D), F32),
            pltpu.SemaphoreType.DMA((9,)),
            pltpu.SemaphoreType.DMA((KINDS,)),
            pltpu.SemaphoreType.DMA((SEMS,)),
        ],
        compiler_params=pltpu.CompilerParams(
            collective_id=0, has_side_effects=True, vmem_limit_bytes=40 * 2**20
        ),
    )(pin(hidden), pin(prob), counts, pin(down_weight), pin(cotangent))
    results = (output, grad_hidden, grad_prob, grad_weight)
    return pl.pallas_call(
        hand_over,
        name="hand_over",
        out_shape=tuple(jax.ShapeDtypeStruct(a.shape, a.dtype) for a in results),
        in_specs=[pl.BlockSpec(memory_space=pltpu.VMEM)] * 4,
        out_specs=(free,) * 4,
        scratch_shapes=[pltpu.SemaphoreType.DMA((4,))],
        compiler_params=pltpu.CompilerParams(vmem_limit_bytes=8 * 2**20),
    )(*results)


def solution(mesh):
    placed = (
        P(("rep", "shard"), None),
        P(("rep", "shard")),
        P(("rep", "shard")),
        P("shard", None),
        P(("rep", "shard"), None),
    )
    return jax.shard_map(
        body,
        mesh=mesh,
        in_specs=placed,
        out_specs=(
            P(("rep", "shard"), None),
            P(("rep", "shard"), None),
            P(("rep", "shard")),
            P("shard", None),
        ),
        check_vma=False,
    )
```
